512 devices in a mesh: rows: 32 (over y, x_hi, core), ctr: 16 (over z, x_lo).
Axes of the slice: x: 4 (x_hi: 2, x_lo: 2; x = x_hi * 2 + x_lo), y: 8, z: 8, core: 2. Of those that a mesh axis runs over, the one named last changes fastest.
Arguments:
- points: bfloat16 [32768, 1024], P('rows'), may hold values from -24 to 24
- centers: bfloat16 [8192, 1024], P('ctr'), may hold values from -6 to 6
- assignment: int32 [32768], P('rows'), may hold values from 0 to 8191, as said below
- row_weight: float32 [32768], P('rows'), may hold values from 0.25 to 4
Outputs:
- row_share: float32 [32768], P(('rows', 'ctr'))
- centroid: float32 [8192, 1024], P(('ctr', 'rows'))
- cluster_share: float32 [8192], P(('ctr', 'rows'))
The draws below stay inside these ranges and needn't reach their ends.
Inputs may be any that keep to these rules, and one draw needn't show every extreme that they name: Row i belongs to cluster assignment[i]. In each aligned block of 1024 rows, at most 4 rows name clusters of any one aligned run of 16 clusters (r * 16 to r * 16 + 15); one such run holds exactly 4 rows of every block.
All inputs are finite; a program needn't handle non-finite values.
Results may differ from the reference program's by a relative error of at most 0.0025.
Values may be sent and summed in bfloat16 or wider, within the bound.
A program may use at most 64 MiB of HBM per device.

```python
import math
import jax
import jax.numpy as jnp
from jax import lax

D = 1024
K = 8192
ROW_DEV = 1024
TOTAL_ROWS = 32768
UNITS = 512
KO = 16
CAP = 4


def shared_centers(key):
    key = jax.random.fold_in(key, 101)
    return jnp.clip(jax.random.normal(key, (K, D), jnp.float32), -6.0, 6.0)


def shared_assignment(key):
    key = jax.random.fold_in(key, 202)
    slab_total = TOTAL_ROWS // ROW_DEV
    full_run = jax.random.randint(jax.random.fold_in(key, 1), (), 0, UNITS).astype(jnp.int32)
    spare_slots = (UNITS - 1) * CAP
    pool_base = jnp.arange(spare_slots, dtype=jnp.int32) // CAP
    run_pool = pool_base + (pool_base >= full_run).astype(jnp.int32)

    def one_slab(slab_key):
        picked = jax.random.permutation(jax.random.fold_in(slab_key, 1), spare_slots)[:ROW_DEV - CAP]
        run_ids = jnp.concatenate([jnp.full((CAP,), full_run, jnp.int32), run_pool[picked]])
        run_ids = run_ids[jax.random.permutation(jax.random.fold_in(slab_key, 2), ROW_DEV)]
        member = jax.random.randint(jax.random.fold_in(slab_key, 3), (ROW_DEV,), 0, KO).astype(jnp.int32)
        return run_ids * KO + member
    slab_keys = jax.random.split(jax.random.fold_in(key, 2), slab_total)
    return jax.vmap(one_slab)(slab_keys).reshape(TOTAL_ROWS).astype(jnp.int32)


def draw_assignment(key, part):
    return shared_assignment(key)


def draw_centers(key, part):
    return shared_centers(key).astype(jnp.bfloat16)


def draw_points(key, part):
    centers = shared_centers(key)
    assigned = shared_assignment(key)
    key = jax.random.fold_in(key, 303)
    is_stale = jax.random.randint(jax.random.fold_in(key, 1), (TOTAL_ROWS,), 0, 4) == 0
    random_source = jax.random.randint(jax.random.fold_in(key, 2), (TOTAL_ROWS,), 0, K).astype(jnp.int32)
    source_ids = jnp.where(is_stale, random_source, assigned)
    slab_pos = (jnp.arange(TOTAL_ROWS) // ROW_DEV).astype(jnp.float32)
    slab_span = float(max(TOTAL_ROWS // ROW_DEV - 1, 1))
    spread = 3.0 ** (0.5 * slab_pos / slab_span)
    scale = jnp.exp(jax.random.uniform(jax.random.fold_in(key, 3), (TOTAL_ROWS,), jnp.float32, math.log(0.1), math.log(1.0)))
    noise = jnp.clip(jax.random.normal(jax.random.fold_in(key, 4), (TOTAL_ROWS, D), jnp.float32), -5.0, 5.0)
    column = jnp.exp(jax.random.uniform(jax.random.fold_in(key, 5), (D,), jnp.float32, math.log(0.5), math.log(2.0)))
    values = centers[source_ids] + (scale * spread)[:, None] * column[None, :] * noise
    return values.astype(jnp.bfloat16)


def steps_of(own_key, extent, shards, least, high):
    gain = 1.0
    for axis_at, blocks in shards:
        heights = jax.random.uniform(jax.random.fold_in(jax.random.fold_in(own_key, 6), axis_at), (blocks,), jnp.float32, least / len(shards), high / len(shards))
        gain = gain * jnp.repeat(jnp.exp(heights), extent[axis_at] // blocks).reshape((-1,) + (1,) * (len(extent) - 1 - axis_at))
    return gain


def setup_inputs(seed: int = 0) -> dict:
    splits = jax.random.split(jax.random.key(seed), 5)
    return {
        "points": draw_points(jax.random.fold_in(splits[4], 71), 0),
        "centers": draw_centers(jax.random.fold_in(splits[4], 71), 0),
        "assignment": draw_assignment(jax.random.fold_in(splits[4], 71), 0),
        "row_weight": jnp.clip(jnp.exp(math.log(4.0) - 2.7725887 * jax.random.uniform(splits[3], (TOTAL_ROWS,), jnp.float32) ** steps_of(splits[3], (TOTAL_ROWS,), ((0, 32),), -0.2, 0.2)), 0.25, 4.0),
    }


def reference(points, centers, assignment, row_weight):
    total_rows = points.shape[0]
    center_norm = jnp.sum(jnp.square(centers.astype(jnp.float32)), axis=1)
    slab_view = points.reshape(total_rows // ROW_DEV, ROW_DEV, D)

    def slab_minimum(slab_block):
        point_norm = jnp.sum(jnp.square(slab_block.astype(jnp.float32)), axis=1)
        cross_term = jnp.dot(slab_block, centers.T, preferred_element_type=jnp.float32)
        return jnp.min(point_norm[:, None] - 2.0 * cross_term + center_norm[None, :], axis=1)

    nearest = lax.map(slab_minimum, slab_view).reshape(total_rows)
    weighted_points = (points.astype(jnp.float32) * row_weight[:, None]).astype(jnp.bfloat16)
    weighted_points = lax.optimization_barrier(weighted_points)
    coord_sums = jax.ops.segment_sum(weighted_points.astype(jnp.float32), assignment, num_segments=K)
    counts = jax.ops.segment_sum(row_weight, assignment, num_segments=K)
    weighted_cost = nearest * row_weight
    cluster_costs = jax.ops.segment_sum(weighted_cost, assignment, num_segments=K)
    mean_cost = jnp.sum(weighted_cost) / jnp.sum(row_weight)
    cluster_size = jnp.maximum(counts, 1.0)
    centroid = coord_sums / cluster_size[:, None]
    cluster_share = cluster_costs / (cluster_size * mean_cost)
    row_share = nearest / mean_cost + 2.0 * cluster_share[assignment]
    return (row_share, centroid, cluster_share)
```

```python
import functools

import jax
import jax.numpy as jnp
from jax import lax
from jax.experimental import pallas as pl
from jax.experimental.pallas import tpu as pltpu
from jax.sharding import PartitionSpec as P

KO = 16
CAP = 4
LANES = 128
MESH = pl.DeviceIdType.MESH
F32 = jnp.float32
BF16 = jnp.bfloat16


def iota(shape, dim):
    return lax.broadcasted_iota(jnp.int32, shape, dim)


def dot_nt(a, b):
    return lax.dot_general(a, b, (((1,), (1,)), ((), ())), preferred_element_type=F32)


def dot_nn(a, b):
    return lax.dot_general(a, b, (((1,), (0,)), ((), ())), preferred_element_type=F32)


def split3(x):
    hi = x.astype(BF16).astype(F32)
    mid = (x - hi).astype(BF16).astype(F32)
    lo = ((x - hi) - mid).astype(BF16).astype(F32)
    return [hi, mid, lo]


def spread(parts):
    stack = jnp.concatenate(parts, axis=0)
    block = iota(stack.shape, 0) & 7
    return jnp.concatenate([jnp.where(block == b, stack, 0.0) for b in range(8)], axis=1).astype(BF16)


def group_sum(x):
    lane = iota(x.shape, 1)
    x = x + jnp.where(lane & 1 == 0, pltpu.roll(x, LANES - 1, 1), pltpu.roll(x, 1, 1))
    return x + jnp.where(lane & 2 == 0, pltpu.roll(x, LANES - 2, 1), pltpu.roll(x, 2, 1))


def kernel(
    n_rows,
    n_ctr,
    points_hbm,
    centers_hbm,
    assign_ref,
    weight_ref,
    row_share_ref,
    centroid_ref,
    share_ref,
    points,
    centers,
    pick,
    rows_out,
    rows_in,
    min_out,
    min_in,
    slot_out,
    slot_in,
    back_out,
    back_in,
    near_ref,
    ids_ref,
    load_sem,
    rows_sems,
    min_sems,
    slot_sems,
    back_sems,
):
    s = lax.axis_index("rows")
    c = lax.axis_index("ctr")
    chunk = points.shape[0] // 4

    center_load = pltpu.make_async_copy(centers_hbm, centers, load_sem.at[4])
    center_load.start()
    point_loads = []
    for q in range(4):
        part = pl.ds(q * chunk, chunk)
        load = pltpu.make_async_copy(points_hbm.at[part], points.at[part], load_sem.at[q])
        load.start()
        point_loads.append(load)

    def row_peers(act):
        def step(d, carry):
            act(lax.rem(s + d, n_rows))
            return carry

        lax.fori_loop(1, n_rows, step, 0)

    def ctr_peers(act):
        def step(d, carry):
            act(lax.rem(c + d, n_ctr))
            return carry

        lax.fori_loop(1, n_ctr, step, 0)

    barrier = pltpu.get_barrier_semaphore()
    row_peers(lambda r: pl.semaphore_signal(barrier, inc=1, device_id=(r, c), device_id_type=MESH))
    ctr_peers(lambda p: pl.semaphore_signal(barrier, inc=1, device_id=(s, p), device_id_type=MESH))

    assign = assign_ref[...]
    weight = weight_ref[...]
    run = (assign >> 4) - c * n_rows
    member = (assign & (KO - 1)).astype(F32)
    hot = [(run[b : b + 1, :] == iota((n_rows, LANES), 0)).astype(F32) for b in range(8)]
    before = jnp.concatenate(
        [
            (iota((LANES, LANES), 0) < iota((LANES, LANES), 1)).astype(F32),
            jnp.ones((LANES, LANES), F32),
        ],
        axis=1,
    ).astype(BF16)
    counted = dot_nn(jnp.concatenate(hot, axis=0).astype(BF16), before)
    carry = jnp.zeros((n_rows, LANES), F32)
    for b in range(8):
        rank = counted[b * n_rows : (b + 1) * n_rows, :LANES] + carry
        carry = carry + counted[b * n_rows : (b + 1) * n_rows, LANES:]
        rank = jnp.sum(hot[b] * rank, axis=0, keepdims=True).astype(jnp.int32)
        here = run[b : b + 1, :]
        code = jnp.where((here >= 0) & (here < n_rows), here * CAP + rank, -1)
        lanes = pl.ds(b * LANES, LANES)
        pick[0:LANES, lanes] = (iota((LANES, LANES), 0) == code).astype(F32).astype(BF16)
        at = iota((2 * LANES, LANES), 0)
        at = (at >> 3) * CAP + (at & (CAP - 1))
        pick[LANES : 3 * LANES, lanes] = (at == code).astype(F32).astype(BF16)

    traits = spread([member + 1.0] + split3(weight))
    picked = dot_nt(traits, pick[0:LANES, :])
    slot_id = jnp.sum(picked[0:8], axis=0, keepdims=True) - 1.0
    slot_weight = jnp.sum(picked[8:32], axis=0, keepdims=True)
    slot_out[:, 0:LANES] = slot_id
    slot_out[:, LANES : 2 * LANES] = slot_weight
    slot_out[:, 2 * LANES : 3 * LANES] = jnp.sum(weight, axis=0, keepdims=True)

    row_weight = jnp.sum(dot_nt(pick[LANES : 3 * LANES, :], traits[8:32]), axis=1, keepdims=True)
    for load in point_loads:
        load.wait()
    half = (iota((2 * LANES, 256), 0) >> 2) & 1
    tiles = []
    for t in range(2):
        low = dot_nn(pick[LANES : 3 * LANES, :], points[:, pl.ds(2 * t * 256, 256)])
        high = dot_nn(pick[LANES : 3 * LANES, :], points[:, pl.ds((2 * t + 1) * 256, 256)])
        tiles.append((jnp.where(half == 0, low, high) * row_weight).reshape(n_rows, 8, 256))
    rows_out[...] = jnp.concatenate(tiles, axis=1).astype(BF16)

    center_load.wait()
    wide = centers[...].astype(F32)
    half_norm = 0.5 * jnp.sum(wide * wide, axis=1, keepdims=True)
    norms = []
    for q in range(4):
        some = points[q * chunk : (q + 1) * chunk, :]
        wide = some.astype(F32)
        wide = wide * wide
        total = wide[:, 0:LANES]
        for k in range(1, 8):
            total = total + wide[:, k * LANES : (k + 1) * LANES]
        norm = jnp.sum(total.T, axis=0, keepdims=True)
        least = jnp.min(half_norm - dot_nt(centers[...], some), axis=0, keepdims=True)
        for k in range(2):
            min_out[2 * q + k : 2 * q + k + 1, :] = least[:, k * LANES : (k + 1) * LANES]
            near_ref[2 * q + k : 2 * q + k + 1, :] = norm[:, k * LANES : (k + 1) * LANES]

    pl.semaphore_wait(barrier, n_rows + n_ctr - 2)

    def send_min(p):
        return pltpu.make_async_remote_copy(
            min_out, min_in.at[c], min_sems.at[0], min_sems.at[1], device_id=(s, p), device_id_type=MESH
        )

    def send_rows(r):
        return pltpu.make_async_remote_copy(
            rows_out.at[r], rows_in.at[s], rows_sems.at[0], rows_sems.at[1], device_id=(r, c), device_id_type=MESH
        )

    def send_slot(r):
        return pltpu.make_async_remote_copy(
            slot_out, slot_in.at[s], slot_sems.at[0], slot_sems.at[1], device_id=(r, c), device_id_type=MESH
        )

    def send_back(p):
        return pltpu.make_async_remote_copy(
            back_out.at[p // 2], back_in.at[c], back_sems.at[0], back_sems.at[1], device_id=(s, p), device_id_type=MESH
        )

    def wait_all(ref, count, sem):
        whole = ref.at[pl.ds(0, count)]
        pltpu.make_async_copy(whole, whole, sem).wait()

    ctr_peers(lambda p: send_min(p).start())
    row_peers(lambda r: send_rows(r).start())
    min_in[c] = min_out[...]
    rows_in[s] = rows_out[s]

    wait_all(min_in, n_ctr - 1, min_sems.at[1])
    near = near_ref[...] + 2.0 * jnp.min(min_in[...], axis=0)
    near_ref[...] = near
    cost = near * weight
    picked = dot_nt(spread(split3(cost)), pick[0:LANES, :])
    slot_out[:, 3 * LANES : 4 * LANES] = jnp.sum(picked, axis=0, keepdims=True)
    slot_out[:, 4 * LANES : 5 * LANES] = jnp.sum(cost, axis=0, keepdims=True)
    row_peers(lambda r: send_slot(r).start())
    slot_in[s] = slot_out[...]

    wait_all(slot_in, n_rows - 1, slot_sems.at[1])
    labels = iota((KO, LANES), 0).astype(F32)
    counts = jnp.zeros((KO, LANES), F32)
    costs = jnp.zeros((KO, LANES), F32)
    sums = jnp.zeros((1, LANES), F32)
    weights = jnp.zeros((1, LANES), F32)
    for r in range(n_rows):
        ids = slot_in[r, :, 0:LANES]
        mine = ids == labels
        counts = counts + jnp.where(mine, slot_in[r, :, LANES : 2 * LANES], 0.0)
        costs = costs + jnp.where(mine, slot_in[r, :, 3 * LANES : 4 * LANES], 0.0)
        weights = weights + slot_in[r, :, 2 * LANES : 3 * LANES]
        sums = sums + slot_in[r, :, 4 * LANES : 5 * LANES]
        ids_ref[r : r + 1, :] = ids
    mean = jnp.sum(sums, axis=1, keepdims=True) / jnp.sum(weights, axis=1, keepdims=True)
    size = jnp.maximum(group_sum(counts), 1.0)
    share = group_sum(costs) / (size * mean)
    slot_share = jnp.sum(jnp.where(slot_id == labels, share, 0.0), axis=0, keepdims=True)
    parts = jnp.concatenate(split3(slot_share) + [jnp.zeros((5, LANES), F32)], axis=0).astype(BF16)
    back = jnp.sum(dot_nn(parts, pick[0:LANES, :]), axis=0, keepdims=True)
    for b in range(8):
        back_out[b] = back[:, b * LANES : (b + 1) * LANES]
    ctr_peers(lambda p: send_back(p).start())
    back_in[c] = back_out[c // 2]

    own = iota((KO, LANES), 1) == s * CAP
    own_size = jnp.sum(jnp.where(own, size, 0.0), axis=1, keepdims=True)
    own_share = jnp.sum(jnp.where(own, share, 0.0), axis=1, keepdims=True)
    square = iota((KO, LANES), 0) == iota((KO, LANES), 1)
    share_ref[...] = jnp.sum(jnp.where(square, own_share, 0.0), axis=0, keepdims=True)[:, :KO]
    lane = iota((LANES, n_rows * KO), 1)
    at = iota((LANES, n_rows * KO), 0)
    place = (at == s * CAP + (lane & (CAP - 1))).astype(F32).astype(BF16)
    ids = dot_nn(ids_ref[...].astype(BF16), place)
    slab = iota((n_rows, n_rows * KO), 0) == iota((n_rows, n_rows * KO), 1) // KO
    ids = jnp.sum(jnp.where(slab, ids, 0.0), axis=0, keepdims=True).astype(jnp.int32)
    at = iota((4 * KO, n_rows * KO), 0)
    quarter = (iota((4 * KO, n_rows * KO), 1) & (KO - 1)) >> 2
    member = ((at & (KO - 1)) == ids) & ((at >> 4) == quarter)
    member = member.astype(F32).astype(BF16)
    wait_all(rows_in, n_rows - 1, rows_sems.at[1])
    coord = dot_nn(member, rows_in[...].reshape(n_rows * KO, 256))
    for q in range(4):
        centroid_ref[:, q * 256 : (q + 1) * 256] = coord[q * KO : (q + 1) * KO, :] / own_size

    wait_all(back_in, n_ctr - 1, back_sems.at[1])
    total = jnp.sum(back_in[...], axis=0)
    total = near_ref[pl.ds(c // 2, 1), :] / mean + 2.0 * total
    width = row_share_ref.shape[1]
    row_share_ref[...] = jnp.where(c % 2 == 0, total[:, :width], total[:, width : 2 * width])

    wait_all(min_in, n_ctr - 1, min_sems.at[0])
    wait_all(rows_in, n_rows - 1, rows_sems.at[0])
    wait_all(slot_in, n_rows - 1, slot_sems.at[0])
    wait_all(back_in, n_ctr - 1, back_sems.at[0])


def local(points, centers, assignment, row_weight):
    slab_rows, width = points.shape
    block = centers.shape[0]
    n_rows = lax.axis_size("rows")
    n_ctr = lax.axis_size("ctr")
    vmem = pl.BlockSpec(memory_space=pltpu.VMEM)
    hbm = pl.BlockSpec(memory_space=pl.ANY)
    row_share, centroid, share = pl.pallas_call(
        functools.partial(kernel, n_rows, n_ctr),
        out_shape=(
            jax.ShapeDtypeStruct((1, slab_rows // n_ctr), F32),
            jax.ShapeDtypeStruct((KO, width), F32),
            jax.ShapeDtypeStruct((1, KO), F32),
        ),
        in_specs=[hbm, hbm, vmem, vmem],
        out_specs=(vmem, vmem, vmem),
        scratch_shapes=[
            pltpu.VMEM((slab_rows, width), BF16),
            pltpu.VMEM((block, width), BF16),
            pltpu.VMEM((3 * LANES, slab_rows), BF16),
            pltpu.VMEM((n_rows, 16, 256), BF16),
            pltpu.VMEM((n_rows, 16, 256), BF16),
            pltpu.VMEM((8, LANES), F32),
            pltpu.VMEM((n_ctr, 8, LANES), F32),
            pltpu.VMEM((1, 5 * LANES), F32),
            pltpu.VMEM((n_rows, 1, 5 * LANES), F32),
            pltpu.VMEM((8, 1, LANES), F32),
            pltpu.VMEM((n_ctr, 1, LANES), F32),
            pltpu.VMEM((8, LANES), F32),
            pltpu.VMEM((n_rows, LANES), F32),
            pltpu.SemaphoreType.DMA((5,)),
            pltpu.SemaphoreType.DMA((2,)),
            pltpu.SemaphoreType.DMA((2,)),
            pltpu.SemaphoreType.DMA((2,)),
            pltpu.SemaphoreType.DMA((2,)),
        ],
        compiler_params=pltpu.CompilerParams(
            collective_id=0, has_side_effects=True, vmem_limit_bytes=48 * 1024 * 1024
        ),
        cost_estimate=pl.CostEstimate(
            flops=2 * slab_rows * width * (block + 3 * LANES),
            bytes_accessed=2 * (slab_rows + block) * width,
            transcendentals=0,
        ),
    )(points, centers, assignment.reshape(8, LANES), row_weight.reshape(8, LANES))
    return row_share.reshape(-1), centroid, share.reshape(-1)


def solution(mesh):
    placed = (P("rows", None), P("ctr", None), P("rows"), P("rows"))
    return jax.shard_map(
        local,
        mesh=mesh,
        in_specs=placed,
        out_specs=(P(("rows", "ctr")), P(("ctr", "rows"), None), P(("ctr", "rows"))),
        check_vma=False,
    )
```

```python
import functools

import jax
import jax.numpy as jnp
from jax import lax
from jax.experimental import pallas as pl
from jax.experimental.pallas import tpu as pltpu
from jax.sharding import PartitionSpec as P

KO = 16
CAP = 4
LANES = 128
MESH = pl.DeviceIdType.MESH
F32 = jnp.float32
BF16 = jnp.bfloat16
IDS = jnp.int16


def iota(shape, dim):
    return lax.broadcasted_iota(jnp.int32, shape, dim)


def dot_nt(a, b):
    return lax.dot_general(a, b, (((1,), (1,)), ((), ())), preferred_element_type=F32)


def dot_nn(a, b):
    return lax.dot_general(a, b, (((1,), (0,)), ((), ())), preferred_element_type=F32)


def split3(x):
    hi = x.astype(BF16).astype(F32)
    mid = (x - hi).astype(BF16).astype(F32)
    lo = ((x - hi) - mid).astype(BF16).astype(F32)
    return [hi, mid, lo]


def spread(parts):
    stack = jnp.concatenate(parts, axis=0)
    block = iota(stack.shape, 0) & 7
    return jnp.concatenate([jnp.where(block == b, stack, 0.0) for b in range(8)], axis=1).astype(BF16)


def kernel(
    n_rows,
    n_ctr,
    points_hbm,
    centers_hbm,
    assign_hbm,
    weight_hbm,
    row_share_ref,
    centroid_ref,
    share_ref,
    points,
    centers,
    assign_ref,
    weight_ref,
    pick,
    rows_out,
    rows_in,
    min_out,
    min_in,
    ids_out,
    ids_in,
    label_out,
    label_in,
    weight_out,
    weight_in,
    cost_out,
    cost_in,
    wide_ids,
    labels,
    near_ref,
    load_sem,
    send_sems,
    recv_sems,
    cost_sems,
):
    s = lax.axis_index("rows")
    c = lax.axis_index("ctr")
    chunk = points.shape[0] // 4
    n_own = row_share_ref.shape[1]

    def row_peer(d):
        k = d // 4
        away = ((k + 1) // 2) * (2 * (k % 2) - 1)
        low = lax.rem(s + d, 4)
        r = lax.rem(s // 4 + away + n_rows // 4, n_rows // 4) * 4 + low
        other = lax.rem(low // 2 + lax.rem(s, 4) // 2, 2)
        return r, c + other * (1 - 2 * lax.rem(c, 2))

    def row_peers(act):
        def step(d, carry):
            act(row_peer(n_rows - d))
            return carry

        lax.fori_loop(1, n_rows, step, 0)

    def ctr_peers(act):
        def step(d, carry):
            act(lax.rem(c + d, n_ctr))
            return carry

        lax.fori_loop(1, n_ctr, step, 0)

    barrier = pltpu.get_barrier_semaphore()
    ctr_peers(lambda p: pl.semaphore_signal(barrier, inc=1, device_id=(s, p), device_id_type=MESH))
    row_peers(lambda to: pl.semaphore_signal(barrier, inc=1, device_id=to, device_id_type=MESH))

    center_load = pltpu.make_async_copy(centers_hbm, centers, load_sem.at[4])
    center_load.start()
    point_loads = []
    for q in range(4):
        part = pl.ds(q * chunk, chunk)
        load = pltpu.make_async_copy(points_hbm.at[part], points.at[part], load_sem.at[q])
        load.start()
        point_loads.append(load)
    assign_load = pltpu.make_async_copy(assign_hbm, assign_ref, load_sem.at[5])
    assign_load.start()
    weight_load = pltpu.make_async_copy(weight_hbm, weight_ref, load_sem.at[6])
    weight_load.start()

    assign_load.wait()
    weight_load.wait()
    assign = assign_ref[...]
    weight = weight_ref[...]
    for h in range(2):
        ids_out[h] = assign[4 * h : 4 * h + 4].astype(IDS)
        weight_out[h] = weight[4 * h : 4 * h + 4]
    run = (assign >> 4) & (n_rows - 1)
    other = ((run >> 1) + lax.rem(s, 4) // 2) & 1
    run = jnp.where(assign >> 9 == c + other * (1 - 2 * lax.rem(c, 2)), run, -1)
    member = (assign & (KO - 1)).astype(F32)
    hot = [(run[b : b + 1, :] == iota((n_rows, LANES), 0)).astype(F32) for b in range(8)]
    before = jnp.concatenate(
        [
            (iota((LANES, LANES), 0) < iota((LANES, LANES), 1)).astype(F32),
            jnp.ones((LANES, LANES), F32),
        ],
        axis=1,
    ).astype(BF16)
    counted = dot_nn(jnp.concatenate(hot, axis=0).astype(BF16), before)
    carry = jnp.zeros((n_rows, LANES), F32)
    for b in range(8):
        rank = counted[b * n_rows : (b + 1) * n_rows, :LANES] + carry
        carry = carry + counted[b * n_rows : (b + 1) * n_rows, LANES:]
        rank = jnp.sum(hot[b] * rank, axis=0, keepdims=True).astype(jnp.int32)
        here = run[b : b + 1, :]
        code = jnp.where(here >= 0, here * CAP + rank, -1)
        lanes = pl.ds(b * LANES, LANES)
        pick[0:LANES, lanes] = (iota((LANES, LANES), 0) == code).astype(F32).astype(BF16)
        at = iota((2 * LANES, LANES), 0)
        at = (at >> 3) * CAP + (at & (CAP - 1))
        pick[LANES : 3 * LANES, lanes] = (at == code).astype(F32).astype(BF16)

    traits = spread([member + 1.0] + split3(weight))
    label_out[...] = jnp.sum(dot_nt(traits[0:8], pick[0:LANES, :]), axis=0, keepdims=True) - 1.0

    for load in point_loads:
        load.wait()
    row_weight = jnp.sum(dot_nt(pick[LANES : 3 * LANES, :], traits[8:32]), axis=1, keepdims=True)
    half = (iota((2 * LANES, 256), 0) >> 2) & 1
    tiles = []
    for t in range(2):
        low = dot_nn(pick[LANES : 3 * LANES, :], points[:, pl.ds(2 * t * 256, 256)])
        high = dot_nn(pick[LANES : 3 * LANES, :], points[:, pl.ds((2 * t + 1) * 256, 256)])
        tiles.append((jnp.where(half == 0, low, high) * row_weight).reshape(n_rows, 8, 256))
    rows_out[...] = jnp.concatenate(tiles, axis=1).astype(BF16)

    center_load.wait()
    wide = centers[...].astype(F32)
    half_norm = 0.5 * jnp.sum(wide * wide, axis=1, keepdims=True)
    for q in range(4):
        some = points[q * chunk : (q + 1) * chunk, :]
        wide = some.astype(F32)
        wide = wide * wide
        total = wide[:, 0:LANES]
        for k in range(1, 8):
            total = total + wide[:, k * LANES : (k + 1) * LANES]
        norm = jnp.sum(total.T, axis=0, keepdims=True)
        least = jnp.min(half_norm - dot_nt(centers[...], some), axis=0, keepdims=True)
        for k in range(2):
            min_out[2 * q + k : 2 * q + k + 1, :] = least[:, k * LANES : (k + 1) * LANES]
            near_ref[2 * q + k : 2 * q + k + 1, :] = norm[:, k * LANES : (k + 1) * LANES]

    side = iota((LANES, LANES), 0) == iota((LANES, LANES), 1)
    own = assign_ref[pl.ds(c // 2, 1), :].astype(F32)
    own = jnp.sum(jnp.where(side, own, 0.0), axis=1, keepdims=True)
    own = jnp.where(c % 2 == 0, own[:n_own], own[n_own : 2 * n_own])
    first = (c * n_rows + s) * KO
    own = jnp.concatenate([own.astype(jnp.int32), first + iota((KO, 1), 0)], axis=0)
    own = jnp.broadcast_to(own, (n_own + KO, LANES))

    pl.semaphore_wait(barrier, n_rows + n_ctr - 2)

    def copy(src, dst, i, recv, device):
        return pltpu.make_async_remote_copy(
            src, dst, send_sems.at[i], recv, device_id=device, device_id_type=MESH
        )

    def wait_all(ref, count, sem):
        whole = ref.at[pl.ds(0, count)]
        pltpu.make_async_copy(whole, whole, sem).wait()

    ctr_peers(lambda p: copy(min_out, min_in.at[c], 0, recv_sems.at[0], (s, p)).start())
    def send_half(src, dst, i):
        def send(to):
            h = lax.rem(to[0], 2)
            copy(src.at[h], dst.at[h, s], i, recv_sems.at[i], to).start()

        row_peers(send)

    core = lax.rem(s, 2)
    send_half(ids_out, ids_in, 1)
    send_half(weight_out, weight_in, 2)
    row_peers(lambda to: copy(label_out, label_in.at[s], 3, recv_sems.at[3], to).start())
    row_peers(lambda to: copy(rows_out.at[to[0]], rows_in.at[s], 4, recv_sems.at[4], to).start())
    min_in[c] = min_out[...]
    ids_in[core, s] = ids_out[core]
    weight_in[core, s] = weight_out[core]
    label_in[s] = label_out[...]
    rows_in[s] = rows_out[s]

    wait_all(min_in, n_ctr - 1, recv_sems.at[0])
    near = near_ref[...] + 2.0 * jnp.min(min_in[...], axis=0)
    near_ref[...] = near
    cost_out[...] = near * weight
    row_peers(lambda to: copy(cost_out, cost_in.at[s], 5, cost_sems.at[s], to).start())
    cost_in[s] = near * weight

    def add(r, values, sums):
        total, each = sums
        ids = wide_ids[r]
        for b in range(8):
            each = each + jnp.where(ids[b : b + 1, :] == own, values[b : b + 1, :], 0.0)
        return total + values, each

    zeros = (jnp.zeros((8, LANES), F32), jnp.zeros(own.shape, F32))

    def add_weight(r, sums):
        for h in range(2):
            wide_ids[r, 4 * h : 4 * h + 4] = ids_in[h, r].astype(jnp.int32)
        return add(r, jnp.concatenate([weight_in[0, r], weight_in[1, r]], axis=0), sums)

    wait_all(ids_in.at[0], n_rows - 1, recv_sems.at[1])
    wait_all(weight_in.at[0], n_rows - 1, recv_sems.at[2])
    partner = (s + 1 - 2 * core, c)
    give = [
        copy(ids_in.at[core], ids_in.at[core], 6, recv_sems.at[5], partner),
        copy(weight_in.at[core], weight_in.at[core], 7, recv_sems.at[6], partner),
    ]
    for one in give:
        one.start()
    for one in give:
        one.wait_recv()
    weight_sum, size = lax.fori_loop(0, n_rows, add_weight, zeros)
    weight_sum = jnp.sum(weight_sum, keepdims=True)
    size = jnp.maximum(jnp.sum(size, axis=1, keepdims=True), 1.0)

    wait_all(label_in, n_rows - 1, recv_sems.at[3])
    for r in range(n_rows):
        labels[r : r + 1, :] = label_in[r]
    lane = iota((LANES, n_rows * KO), 1)
    at = iota((LANES, n_rows * KO), 0)
    place = (at == s * CAP + (lane & (CAP - 1))).astype(F32).astype(BF16)
    ids = dot_nn(labels[...].astype(BF16), place)
    slab = iota((n_rows, n_rows * KO), 0) == iota((n_rows, n_rows * KO), 1) // KO
    ids = jnp.sum(jnp.where(slab, ids, 0.0), axis=0, keepdims=True).astype(jnp.int32)
    at = iota((4 * KO, n_rows * KO), 0)
    quarter = (iota((4 * KO, n_rows * KO), 1) & (KO - 1)) >> 2
    member = ((at & (KO - 1)) == ids) & ((at >> 4) == quarter)
    member = member.astype(F32).astype(BF16)
    wait_all(rows_in, n_rows - 1, recv_sems.at[4])
    coord = dot_nn(member, rows_in[...].reshape(n_rows * KO, 256))
    for q in range(4):
        centroid_ref[:, q * 256 : (q + 1) * 256] = coord[q * KO : (q + 1) * KO, :] / size[n_own:]

    def add_cost(d, sums):
        r, _ = row_peer(d)
        pltpu.make_async_copy(cost_in.at[r], cost_in.at[r], cost_sems.at[r]).wait()
        return add(r, cost_in[r], sums)

    cost_sum, cost = lax.fori_loop(1, n_rows, add_cost, add(s, cost_in[s], zeros))
    mean = jnp.sum(cost_sum, keepdims=True) / weight_sum
    share = jnp.sum(cost, axis=1, keepdims=True) / (size * mean)
    diagonal = iota(own.shape, 0) == iota(own.shape, 1)
    share = jnp.sum(jnp.where(diagonal, share, 0.0), axis=0, keepdims=True)
    share_ref[...] = share[:, n_own : n_own + KO]
    near = near_ref[pl.ds(c // 2, 1), :]
    near = jnp.where(c % 2 == 0, near[:, :n_own], near[:, n_own : 2 * n_own])
    row_share_ref[...] = near / mean + 2.0 * share[:, :n_own]

    wait_all(min_in, n_ctr - 1, send_sems.at[0])
    wait_all(ids_in.at[0], n_rows - 1, send_sems.at[1])
    wait_all(weight_in.at[0], n_rows - 1, send_sems.at[2])
    for one in give:
        one.wait_send()
    wait_all(label_in, n_rows - 1, send_sems.at[3])
    wait_all(rows_in, n_rows - 1, send_sems.at[4])
    wait_all(cost_in, n_rows - 1, send_sems.at[5])


def deliver(*refs):
    n = len(refs) // 2
    for i in range(n):
        refs[n + i][...] = refs[i][...]


def local(points, centers, assignment, row_weight):
    slab_rows, width = points.shape
    block = centers.shape[0]
    n_rows = lax.axis_size("rows")
    n_ctr = lax.axis_size("ctr")
    vmem = pl.BlockSpec(memory_space=pltpu.VMEM)
    hbm = pl.BlockSpec(memory_space=pltpu.HBM)
    row_share, centroid, share = pl.pallas_call(
        functools.partial(kernel, n_rows, n_ctr),
        out_shape=(
            jax.ShapeDtypeStruct((1, slab_rows // n_ctr), F32),
            jax.ShapeDtypeStruct((KO, width), F32),
            jax.ShapeDtypeStruct((1, KO), F32),
        ),
        in_specs=[hbm, hbm, hbm, hbm],
        out_specs=(vmem, vmem, vmem),
        scratch_shapes=[
            pltpu.VMEM((slab_rows, width), BF16),
            pltpu.VMEM((block, width), BF16),
            pltpu.VMEM((8, LANES), jnp.int32),
            pltpu.VMEM((8, LANES), F32),
            pltpu.VMEM((3 * LANES, slab_rows), BF16),
            pltpu.VMEM((n_rows, 16, 256), BF16),
            pltpu.VMEM((n_rows, 16, 256), BF16),
            pltpu.VMEM((8, LANES), F32),
            pltpu.VMEM((n_ctr, 8, LANES), F32),
            pltpu.VMEM((2, 4, LANES), IDS),
            pltpu.VMEM((2, n_rows, 4, LANES), IDS),
            pltpu.VMEM((1, LANES), F32),
            pltpu.VMEM((n_rows, 1, LANES), F32),
            pltpu.VMEM((2, 4, LANES), F32),
            pltpu.VMEM((2, n_rows, 4, LANES), F32),
            pltpu.VMEM((8, LANES), F32),
            pltpu.VMEM((n_rows, 8, LANES), F32),
            pltpu.VMEM((n_rows, 8, LANES), jnp.int32),
            pltpu.VMEM((n_rows, LANES), F32),
            pltpu.VMEM((8, LANES), F32),
            pltpu.SemaphoreType.DMA((7,)),
            pltpu.SemaphoreType.DMA((8,)),
            pltpu.SemaphoreType.DMA((7,)),
            pltpu.SemaphoreType.DMA((n_rows,)),
        ],
        compiler_params=pltpu.CompilerParams(
            collective_id=0, has_side_effects=True
        ),
        cost_estimate=pl.CostEstimate(
            flops=2 * slab_rows * width * (block + 3 * LANES),
            bytes_accessed=2 * (slab_rows + block) * width,
            transcendentals=0,
        ),
    )(points, centers, assignment.reshape(8, LANES), row_weight.reshape(8, LANES))
    made = (row_share, centroid, share)
    row_share, centroid, share = pl.pallas_call(
        deliver,
        out_shape=tuple(jax.ShapeDtypeStruct(x.shape, x.dtype) for x in made),
        in_specs=[vmem] * 3,
        out_specs=(vmem,) * 3,
    )(*made)
    return row_share.reshape(-1), centroid, share.reshape(-1)


def solution(mesh):
    placed = (P("rows", None), P("ctr", None), P("rows"), P("rows"))
    return jax.shard_map(
        local,
        mesh=mesh,
        in_specs=placed,
        out_specs=(P(("rows", "ctr")), P(("ctr", "rows"), None), P(("ctr", "rows"))),
        check_vma=False,
    )
```

```python
import functools

import jax
import jax.numpy as jnp
from jax import lax
from jax.experimental import pallas as pl
from jax.experimental.pallas import tpu as pltpu
from jax.sharding import PartitionSpec as P

KO = 16
CAP = 4
LANES = 128
MESH = pl.DeviceIdType.MESH
F32 = jnp.float32
BF16 = jnp.bfloat16
IDS = jnp.int16


def iota(shape, dim):
    return lax.broadcasted_iota(jnp.int32, shape, dim)


def dot_nt(a, b):
    return lax.dot_general(a, b, (((1,), (1,)), ((), ())), preferred_element_type=F32)


def dot_nn(a, b):
    return lax.dot_general(a, b, (((1,), (0,)), ((), ())), preferred_element_type=F32)


def split3(x):
    hi = x.astype(BF16).astype(F32)
    mid = (x - hi).astype(BF16).astype(F32)
    lo = ((x - hi) - mid).astype(BF16).astype(F32)
    return [hi, mid, lo]


def spread(parts):
    stack = jnp.concatenate(parts, axis=0)
    block = iota(stack.shape, 0) & 7
    return jnp.concatenate([jnp.where(block == b, stack, 0.0) for b in range(8)], axis=1).astype(BF16)


def kernel(
    n_rows,
    n_ctr,
    points_hbm,
    centers_hbm,
    assign_hbm,
    weight_hbm,
    row_share_ref,
    centroid_ref,
    share_ref,
    points,
    centers,
    assign_ref,
    weight_ref,
    pick,
    rows_out,
    rows_in,
    min_out,
    min_in,
    ids_out,
    ids_in,
    label_out,
    label_in,
    weight_out,
    weight_in,
    cost_out,
    cost_in,
    wide_ids,
    labels,
    near_ref,
    load_sem,
    send_sems,
    recv_sems,
    cost_sems,
    late_sem,
    go_sem,
):
    s = lax.axis_index("rows")
    c = lax.axis_index("ctr")
    chunk = points.shape[0] // 4
    n_own = row_share_ref.shape[1]

    def row_peer(d):
        k = d >> 2
        away = ((k + 1) >> 1) * (2 * (k & 1) - 1)
        low = (s + d) & 3
        r = (((s >> 2) + away) & (n_rows // 4 - 1)) * 4 + low
        other = ((low >> 1) + (s >> 1)) & 1
        return r, c + other * (1 - 2 * (c & 1))

    def row_peers(act, unroll=False):
        if unroll:
            for d in range(n_rows - 1, 0, -1):
                act(row_peer(d))
            return

        def step(d, carry):
            act(row_peer(n_rows - d))
            return carry

        lax.fori_loop(1, n_rows, step, 0)

    half = n_ctr // 2

    def early_peers(act):
        for d in sorted(range(half), key=lambda d: abs(2 * d - half)):
            p = (c + d) & (half - 1)
            pl.when(p != c)(functools.partial(act, p))

    def late_peers(act):
        for d in range(half):
            p = half + ((c + d) & (half - 1))
            pl.when(p != c)(functools.partial(act, p))

    barrier = pltpu.get_barrier_semaphore()
    assign_load = pltpu.make_async_copy(assign_hbm, assign_ref, load_sem.at[5])
    assign_load.start()
    weight_load = pltpu.make_async_copy(weight_hbm, weight_ref, load_sem.at[6])
    weight_load.start()

    center_load = pltpu.make_async_copy(centers_hbm, centers, load_sem.at[4])
    center_load.start()
    point_loads = []
    for q in range(4):
        part = pl.ds(q * chunk, chunk)
        load = pltpu.make_async_copy(points_hbm.at[part], points.at[part], load_sem.at[q])
        load.start()
        point_loads.append(load)

    def enter(p):
        pl.semaphore_signal(barrier, inc=1, device_id=(s, p), device_id_type=MESH)

    @pl.when(c < half)
    def _():
        early_peers(enter)
        late_peers(enter)

    row_peers(lambda to: pl.semaphore_signal(barrier, inc=1, device_id=to, device_id_type=MESH), True)

    assign_load.wait()
    weight_load.wait()
    assign = assign_ref[...]
    weight = weight_ref[...]
    for h in range(2):
        ids_out[h] = assign[4 * h : 4 * h + 4].astype(IDS)
        weight_out[h] = weight[4 * h : 4 * h + 4]
    run = (assign >> 4) & (n_rows - 1)
    other = ((run >> 1) + lax.rem(s, 4) // 2) & 1
    run = jnp.where(assign >> 9 == c + other * (1 - 2 * lax.rem(c, 2)), run, -1)
    member = (assign & (KO - 1)).astype(F32)
    hot = [(run[b : b + 1, :] == iota((n_rows, LANES), 0)).astype(F32) for b in range(8)]
    before = jnp.concatenate(
        [
            (iota((LANES, LANES), 0) < iota((LANES, LANES), 1)).astype(F32),
            jnp.ones((LANES, LANES), F32),
        ],
        axis=1,
    ).astype(BF16)
    counted = dot_nn(jnp.concatenate(hot, axis=0).astype(BF16), before)
    carry = jnp.zeros((n_rows, LANES), F32)
    for b in range(8):
        rank = counted[b * n_rows : (b + 1) * n_rows, :LANES] + carry
        carry = carry + counted[b * n_rows : (b + 1) * n_rows, LANES:]
        rank = jnp.sum(hot[b] * rank, axis=0, keepdims=True).astype(jnp.int32)
        here = run[b : b + 1, :]
        code = jnp.where(here >= 0, here * CAP + rank, -1)
        lanes = pl.ds(b * LANES, LANES)
        pick[0:LANES, lanes] = (iota((LANES, LANES), 0) == code).astype(F32).astype(BF16)
        at = iota((2 * LANES, LANES), 0)
        at = (at >> 3) * CAP + (at & (CAP - 1))
        pick[LANES : 3 * LANES, lanes] = (at == code).astype(F32).astype(BF16)

    traits = spread([member + 1.0] + split3(weight))
    label_out[...] = jnp.sum(dot_nt(traits[0:8], pick[0:LANES, :]), axis=0, keepdims=True) - 1.0

    for load in point_loads:
        load.wait()
    center_load.wait()
    wide = centers[...].astype(F32)
    half_norm = 0.5 * jnp.sum(wide * wide, axis=1, keepdims=True)
    for q in range(4):
        some = points[q * chunk : (q + 1) * chunk, :]
        wide = some.astype(F32)
        wide = wide * wide
        total = wide[:, 0:LANES]
        for k in range(1, 8):
            total = total + wide[:, k * LANES : (k + 1) * LANES]
        norm = jnp.sum(total.T, axis=0, keepdims=True)
        least = jnp.min(half_norm - dot_nt(centers[...], some), axis=0, keepdims=True)
        for k in range(2):
            min_out[2 * q + k : 2 * q + k + 1, :] = least[:, k * LANES : (k + 1) * LANES]
            near_ref[2 * q + k : 2 * q + k + 1, :] = norm[:, k * LANES : (k + 1) * LANES]

    row_weight = jnp.sum(dot_nt(pick[LANES : 3 * LANES, :], traits[8:32]), axis=1, keepdims=True)
    odd = (iota((2 * LANES, 256), 0) >> 2) & 1
    tiles = []
    for t in range(2):
        low = dot_nn(pick[LANES : 3 * LANES, :], points[:, pl.ds(2 * t * 256, 256)])
        high = dot_nn(pick[LANES : 3 * LANES, :], points[:, pl.ds((2 * t + 1) * 256, 256)])
        tiles.append((jnp.where(odd == 0, low, high) * row_weight).reshape(n_rows, 8, 256))
    rows_out[...] = jnp.concatenate(tiles, axis=1).astype(BF16)

    side = iota((LANES, LANES), 0) == iota((LANES, LANES), 1)
    own = assign_ref[pl.ds(c // 2, 1), :].astype(F32)
    own = jnp.sum(jnp.where(side, own, 0.0), axis=1, keepdims=True)
    own = jnp.where(c % 2 == 0, own[:n_own], own[n_own : 2 * n_own])
    first = (c * n_rows + s) * KO
    own = jnp.concatenate([own.astype(jnp.int32), first + iota((KO, 1), 0)], axis=0)
    own = jnp.broadcast_to(own, (n_own + KO, LANES))

    pl.semaphore_wait(barrier, n_rows + half - 2 + c // half)

    def copy(src, dst, i, recv, device):
        return pltpu.make_async_remote_copy(
            src, dst, send_sems.at[i], recv, device_id=device, device_id_type=MESH
        )

    def wait_all(ref, count, sem):
        whole = ref.at[pl.ds(0, count)]
        pltpu.make_async_copy(whole, whole, sem).wait()

    def send_min(p):
        copy(min_out, min_in.at[c], 0, recv_sems.at[0], (s, p)).start()

    def tell_late(p):
        pl.semaphore_signal(late_sem, inc=1, device_id=(s, p), device_id_type=MESH)

    early_peers(send_min)

    @pl.when(c >= half)
    def _():
        early_peers(tell_late)

    def send_half(src, dst, i):
        def send(to):
            h = to[0] & 1
            copy(src.at[h], dst.at[h, s], i, recv_sems.at[i], to).start()

        row_peers(send)

    core = s & 1
    send_half(ids_out, ids_in, 1)
    send_half(weight_out, weight_in, 2)
    row_peers(lambda to: copy(label_out, label_in.at[s], 3, recv_sems.at[3], to).start())
    row_peers(lambda to: copy(rows_out.at[to[0]], rows_in.at[s], 4, recv_sems.at[4], to).start())
    min_in[c] = min_out[...]
    ids_in[core, s] = ids_out[core]
    weight_in[core, s] = weight_out[core]
    label_in[s] = label_out[...]
    rows_in[s] = rows_out[s]

    @pl.when(c >= half)
    def _():
        pl.semaphore_wait(go_sem, 1)
        late_peers(send_min)

    wait_all(min_in, n_ctr - 1, recv_sems.at[0])
    near = near_ref[...] + 2.0 * jnp.min(min_in[...], axis=0)
    near_ref[...] = near
    cost_out[...] = near * weight
    row_peers(lambda to: copy(cost_out, cost_in.at[s], 5, cost_sems.at[s], to).start(), True)
    cost_in[s] = near * weight

    @pl.when(c < half)
    def _():
        pl.semaphore_wait(late_sem, half)
        mirror = n_ctr - 2 - 2 * (c // 2) + c % 2
        pl.semaphore_signal(go_sem, inc=1, device_id=(s, mirror), device_id_type=MESH)
        late_peers(send_min)

    def add(r, values, sums):
        total, each = sums
        ids = wide_ids[r]
        for b in range(8):
            each = each + jnp.where(ids[b : b + 1, :] == own, values[b : b + 1, :], 0.0)
        return total + values, each

    zeros = (jnp.zeros((8, LANES), F32), jnp.zeros(own.shape, F32))

    def add_weight(r, sums):
        for h in range(2):
            wide_ids[r, 4 * h : 4 * h + 4] = ids_in[h, r].astype(jnp.int32)
        return add(r, jnp.concatenate([weight_in[0, r], weight_in[1, r]], axis=0), sums)

    wait_all(ids_in.at[0], n_rows - 1, recv_sems.at[1])
    wait_all(weight_in.at[0], n_rows - 1, recv_sems.at[2])
    partner = (s + 1 - 2 * core, c)
    give = [
        copy(ids_in.at[core], ids_in.at[core], 6, recv_sems.at[5], partner),
        copy(weight_in.at[core], weight_in.at[core], 7, recv_sems.at[6], partner),
    ]
    for one in give:
        one.start()
    for one in give:
        one.wait_recv()
    weight_sum, size = lax.fori_loop(0, n_rows, add_weight, zeros)
    weight_sum = jnp.sum(weight_sum, keepdims=True)
    size = jnp.maximum(jnp.sum(size, axis=1, keepdims=True), 1.0)

    wait_all(label_in, n_rows - 1, recv_sems.at[3])
    for r in range(n_rows):
        labels[r : r + 1, :] = label_in[r]
    lane = iota((LANES, n_rows * KO), 1)
    at = iota((LANES, n_rows * KO), 0)
    place = (at == s * CAP + (lane & (CAP - 1))).astype(F32).astype(BF16)
    ids = dot_nn(labels[...].astype(BF16), place)
    slab = iota((n_rows, n_rows * KO), 0) == iota((n_rows, n_rows * KO), 1) // KO
    ids = jnp.sum(jnp.where(slab, ids, 0.0), axis=0, keepdims=True).astype(jnp.int32)
    at = iota((4 * KO, n_rows * KO), 0)
    quarter = (iota((4 * KO, n_rows * KO), 1) & (KO - 1)) >> 2
    member = ((at & (KO - 1)) == ids) & ((at >> 4) == quarter)
    member = member.astype(F32).astype(BF16)
    wait_all(rows_in, n_rows - 1, recv_sems.at[4])
    coord = dot_nn(member, rows_in[...].reshape(n_rows * KO, 256))
    for q in range(4):
        centroid_ref[:, q * 256 : (q + 1) * 256] = coord[q * KO : (q + 1) * KO, :] / size[n_own:]

    def add_cost(d, sums):
        r, _ = row_peer(d)
        pltpu.make_async_copy(cost_in.at[r], cost_in.at[r], cost_sems.at[r]).wait()
        return add(r, cost_in[r], sums)

    cost_sum, cost = lax.fori_loop(1, n_rows, add_cost, add(s, cost_in[s], zeros))
    mean = jnp.sum(cost_sum, keepdims=True) / weight_sum
    share = jnp.sum(cost, axis=1, keepdims=True) / (size * mean)
    diagonal = iota(own.shape, 0) == iota(own.shape, 1)
    share = jnp.sum(jnp.where(diagonal, share, 0.0), axis=0, keepdims=True)
    share_ref[...] = share[:, n_own : n_own + KO]
    near = near_ref[pl.ds(c // 2, 1), :]
    near = jnp.where(c % 2 == 0, near[:, :n_own], near[:, n_own : 2 * n_own])
    row_share_ref[...] = near / mean + 2.0 * share[:, :n_own]

    wait_all(min_in, n_ctr - 1, send_sems.at[0])
    wait_all(ids_in.at[0], n_rows - 1, send_sems.at[1])
    wait_all(weight_in.at[0], n_rows - 1, send_sems.at[2])
    for one in give:
        one.wait_send()
    wait_all(label_in, n_rows - 1, send_sems.at[3])
    wait_all(rows_in, n_rows - 1, send_sems.at[4])
    wait_all(cost_in, n_rows - 1, send_sems.at[5])


def deliver(*refs):
    n = len(refs) // 2
    for i in range(n):
        refs[n + i][...] = refs[i][...]


def local(points, centers, assignment, row_weight):
    slab_rows, width = points.shape
    block = centers.shape[0]
    n_rows = lax.axis_size("rows")
    n_ctr = lax.axis_size("ctr")
    vmem = pl.BlockSpec(memory_space=pltpu.VMEM)
    hbm = pl.BlockSpec(memory_space=pltpu.HBM)
    row_share, centroid, share = pl.pallas_call(
        functools.partial(kernel, n_rows, n_ctr),
        out_shape=(
            jax.ShapeDtypeStruct((1, slab_rows // n_ctr), F32),
            jax.ShapeDtypeStruct((KO, width), F32),
            jax.ShapeDtypeStruct((1, KO), F32),
        ),
        in_specs=[hbm, hbm, hbm, hbm],
        out_specs=(vmem, vmem, vmem),
        scratch_shapes=[
            pltpu.VMEM((slab_rows, width), BF16),
            pltpu.VMEM((block, width), BF16),
            pltpu.VMEM((8, LANES), jnp.int32),
            pltpu.VMEM((8, LANES), F32),
            pltpu.VMEM((3 * LANES, slab_rows), BF16),
            pltpu.VMEM((n_rows, 16, 256), BF16),
            pltpu.VMEM((n_rows, 16, 256), BF16),
            pltpu.VMEM((8, LANES), F32),
            pltpu.VMEM((n_ctr, 8, LANES), F32),
            pltpu.VMEM((2, 4, LANES), IDS),
            pltpu.VMEM((2, n_rows, 4, LANES), IDS),
            pltpu.VMEM((1, LANES), F32),
            pltpu.VMEM((n_rows, 1, LANES), F32),
            pltpu.VMEM((2, 4, LANES), F32),
            pltpu.VMEM((2, n_rows, 4, LANES), F32),
            pltpu.VMEM((8, LANES), F32),
            pltpu.VMEM((n_rows, 8, LANES), F32),
            pltpu.VMEM((n_rows, 8, LANES), jnp.int32),
            pltpu.VMEM((n_rows, LANES), F32),
            pltpu.VMEM((8, LANES), F32),
            pltpu.SemaphoreType.DMA((7,)),
            pltpu.SemaphoreType.DMA((8,)),
            pltpu.SemaphoreType.DMA((7,)),
            pltpu.SemaphoreType.DMA((n_rows,)),
            pltpu.SemaphoreType.REGULAR,
            pltpu.SemaphoreType.REGULAR,
        ],
        compiler_params=pltpu.CompilerParams(
            collective_id=0, has_side_effects=True
        ),
        cost_estimate=pl.CostEstimate(
            flops=2 * slab_rows * width * (block + 3 * LANES),
            bytes_accessed=2 * (slab_rows + block) * width,
            transcendentals=0,
        ),
    )(points, centers, assignment.reshape(8, LANES), row_weight.reshape(8, LANES))
    made = (row_share, centroid, share)
    row_share, centroid, share = pl.pallas_call(
        deliver,
        out_shape=tuple(jax.ShapeDtypeStruct(x.shape, x.dtype) for x in made),
        in_specs=[vmem] * 3,
        out_specs=(vmem,) * 3,
    )(*made)
    return row_share.reshape(-1), centroid, share.reshape(-1)


def solution(mesh):
    placed = (P("rows", None), P("ctr", None), P("rows"), P("rows"))
    return jax.shard_map(
        local,
        mesh=mesh,
        in_specs=placed,
        out_specs=(P(("rows", "ctr")), P(("ctr", "rows"), None), P(("ctr", "rows"))),
        check_vma=False,
    )
```

```python
import functools

import jax
import jax.numpy as jnp
from jax import lax
from jax.experimental import pallas as pl
from jax.experimental.pallas import tpu as pltpu
from jax.sharding import PartitionSpec as P

KO = 16
CAP = 4
LANES = 128
MESH = pl.DeviceIdType.MESH
F32 = jnp.float32
BF16 = jnp.bfloat16
CODE = jnp.int16


def iota(shape, dim):
    return lax.broadcasted_iota(jnp.int32, shape, dim)


def dot_nt(a, b):
    return lax.dot_general(a, b, (((1,), (1,)), ((), ())), preferred_element_type=F32)


def dot_nn(a, b):
    return lax.dot_general(a, b, (((1,), (0,)), ((), ())), preferred_element_type=F32)


def split3(x):
    hi = x.astype(BF16).astype(F32)
    mid = (x - hi).astype(BF16).astype(F32)
    lo = ((x - hi) - mid).astype(BF16).astype(F32)
    return [hi, mid, lo]


def weight_code(x):
    return (((x - 0.25) * (65535 / 3.75) + 0.5).astype(jnp.int32) - 32768).astype(CODE)


def code_weight(code):
    return (code.astype(jnp.int32) + 32768).astype(F32) * (3.75 / 65535) + 0.25


def cost_code(x):
    at = (jnp.log2(jnp.maximum(x, 2.0**-106)) + 106.0) * 512.0 + 0.5
    return (jnp.minimum(at, 65535.0).astype(jnp.int32) - 32768).astype(CODE)


def code_cost(code):
    return jnp.exp2((code.astype(jnp.int32) + 32768).astype(F32) * (1 / 512) - 106.0)


def spread(parts):
    stack = jnp.concatenate(parts, axis=0)
    block = iota(stack.shape, 0) & 7
    return jnp.concatenate([jnp.where(block == b, stack, 0.0) for b in range(8)], axis=1).astype(BF16)


def kernel(
    n_rows,
    n_ctr,
    points_hbm,
    centers_hbm,
    assign_hbm,
    weight_hbm,
    row_share_ref,
    centroid_ref,
    share_ref,
    points,
    centers,
    assign_ref,
    weight_ref,
    pick,
    rows_out,
    rows_in,
    min_out,
    min_in,
    ids_out,
    ids_in,
    label_out,
    label_in,
    cost_out,
    cost_in,
    wide_ids,
    labels,
    near_ref,
    load_sem,
    send_sems,
    recv_sems,
    cost_sems,
    late_sem,
    go_sem,
):
    s = lax.axis_index("rows")
    c = lax.axis_index("ctr")
    chunk = points.shape[0] // 4
    n_own = row_share_ref.shape[1]

    def row_peer(d):
        k = d >> 2
        away = ((k + 1) >> 1) * (2 * (k & 1) - 1)
        low = (s + d) & 3
        r = (((s >> 2) + away) & (n_rows // 4 - 1)) * 4 + low
        other = ((low >> 1) + (s >> 1)) & 1
        return r, c + other * (1 - 2 * (c & 1))

    def row_peers(act, unroll=False):
        if unroll:
            for d in range(n_rows - 1, 0, -1):
                act(row_peer(d))
            return

        def step(d, carry):
            act(row_peer(n_rows - d))
            return carry

        lax.fori_loop(1, n_rows, step, 0)

    half = n_ctr // 2

    def early_peers(act):
        for d in sorted(range(half), key=lambda d: abs(2 * d - half)):
            p = (c + d) & (half - 1)
            pl.when(p != c)(functools.partial(act, p))

    def late_peers(act):
        for d in range(half):
            p = half + ((c + d) & (half - 1))
            pl.when(p != c)(functools.partial(act, p))

    barrier = pltpu.get_barrier_semaphore()
    assign_load = pltpu.make_async_copy(assign_hbm, assign_ref, load_sem.at[5])
    assign_load.start()
    weight_load = pltpu.make_async_copy(weight_hbm, weight_ref, load_sem.at[6])
    weight_load.start()

    center_load = pltpu.make_async_copy(centers_hbm, centers, load_sem.at[4])
    center_load.start()
    point_loads = []
    for q in range(4):
        part = pl.ds(q * chunk, chunk)
        load = pltpu.make_async_copy(points_hbm.at[part], points.at[part], load_sem.at[q])
        load.start()
        point_loads.append(load)

    def enter(p):
        pl.semaphore_signal(barrier, inc=1, device_id=(s, p), device_id_type=MESH)

    @pl.when(c < half)
    def _():
        early_peers(enter)
        late_peers(enter)

    row_peers(lambda to: pl.semaphore_signal(barrier, inc=1, device_id=to, device_id_type=MESH), True)

    def slots():
        assign = assign_ref[...]
        weight = weight_ref[...]
        for h in range(2):
            ids_out[h, 0] = assign[4 * h : 4 * h + 4].astype(CODE)
            ids_out[h, 1] = weight_code(weight[4 * h : 4 * h + 4])
        run = (assign >> 4) & (n_rows - 1)
        other = ((run >> 1) + lax.rem(s, 4) // 2) & 1
        run = jnp.where(assign >> 9 == c + other * (1 - 2 * lax.rem(c, 2)), run, -1)
        member = (assign & (KO - 1)).astype(F32)
        hot = [(run[b : b + 1, :] == iota((n_rows, LANES), 0)).astype(F32) for b in range(8)]
        before = jnp.concatenate(
            [
                (iota((LANES, LANES), 0) < iota((LANES, LANES), 1)).astype(F32),
                jnp.ones((LANES, LANES), F32),
            ],
            axis=1,
        ).astype(BF16)
        counted = dot_nn(jnp.concatenate(hot, axis=0).astype(BF16), before)
        carry = jnp.zeros((n_rows, LANES), F32)
        for b in range(8):
            rank = counted[b * n_rows : (b + 1) * n_rows, :LANES] + carry
            carry = carry + counted[b * n_rows : (b + 1) * n_rows, LANES:]
            rank = jnp.sum(hot[b] * rank, axis=0, keepdims=True).astype(jnp.int32)
            here = run[b : b + 1, :]
            code = jnp.where(here >= 0, here * CAP + rank, -1)
            lanes = pl.ds(b * LANES, LANES)
            pick[0:LANES, lanes] = (iota((LANES, LANES), 0) == code).astype(F32).astype(BF16)
            at = iota((2 * LANES, LANES), 0)
            at = (at >> 3) * CAP + (at & (CAP - 1))
            pick[LANES : 3 * LANES, lanes] = (at == code).astype(F32).astype(BF16)

        traits = spread([member + 1.0] + split3(weight))
        label_out[...] = jnp.sum(dot_nt(traits[0:8], pick[0:LANES, :]), axis=0, keepdims=True) - 1.0

        row_weight = jnp.sum(dot_nt(pick[LANES : 3 * LANES, :], traits[8:32]), axis=1, keepdims=True)
        odd = (iota((2 * LANES, 256), 0) >> 2) & 1
        tiles = []
        for t in range(2):
            low = dot_nn(pick[LANES : 3 * LANES, :], points[:, pl.ds(2 * t * 256, 256)])
            high = dot_nn(pick[LANES : 3 * LANES, :], points[:, pl.ds((2 * t + 1) * 256, 256)])
            tiles.append((jnp.where(odd == 0, low, high) * row_weight).reshape(n_rows, 8, 256))
        rows_out[...] = jnp.concatenate(tiles, axis=1).astype(BF16)

    assign_load.wait()
    weight_load.wait()
    for load in point_loads:
        load.wait()
    pl.when(c < half)(slots)

    center_load.wait()
    wide = centers[...].astype(F32)
    half_norm = 0.5 * jnp.sum(wide * wide, axis=1, keepdims=True)
    for q in range(4):
        some = points[q * chunk : (q + 1) * chunk, :]
        wide = some.astype(F32)
        wide = wide * wide
        total = wide[:, 0:LANES]
        for k in range(1, 8):
            total = total + wide[:, k * LANES : (k + 1) * LANES]
        norm = jnp.sum(total.T, axis=0, keepdims=True)
        least = jnp.min(half_norm - dot_nt(centers[...], some), axis=0, keepdims=True)
        for k in range(2):
            min_out[2 * q + k : 2 * q + k + 1, :] = least[:, k * LANES : (k + 1) * LANES]
            near_ref[2 * q + k : 2 * q + k + 1, :] = norm[:, k * LANES : (k + 1) * LANES]

    pl.semaphore_wait(barrier, n_rows + half - 2 + c // half)

    def copy(src, dst, i, recv, device):
        return pltpu.make_async_remote_copy(
            src, dst, send_sems.at[i], recv, device_id=device, device_id_type=MESH
        )

    def wait_all(ref, count, sem):
        whole = ref.at[pl.ds(0, count)]
        pltpu.make_async_copy(whole, whole, sem).wait()

    def send_min(p):
        copy(min_out, min_in.at[c], 0, recv_sems.at[0], (s, p)).start()

    def tell_late(p):
        pl.semaphore_signal(late_sem, inc=1, device_id=(s, p), device_id_type=MESH)

    early_peers(send_min)

    @pl.when(c >= half)
    def _():
        early_peers(tell_late)
        slots()

    def send_half(src, dst, i):
        def send(to):
            h = to[0] & 1
            copy(src.at[h], dst.at[h, s], i, recv_sems.at[i], to).start()

        row_peers(send)

    core = s & 1
    send_half(ids_out, ids_in, 1)
    row_peers(lambda to: copy(label_out, label_in.at[s], 3, recv_sems.at[3], to).start())
    row_peers(lambda to: copy(rows_out.at[to[0]], rows_in.at[s], 4, recv_sems.at[4], to).start())
    min_in[c] = min_out[...]
    ids_in[core, s] = ids_out[core]
    label_in[s] = label_out[...]
    rows_in[s] = rows_out[s]

    @pl.when(c < half)
    def _():
        pl.semaphore_wait(late_sem, half)
        mirror = n_ctr - 2 - 2 * (c // 2) + c % 2
        pl.semaphore_signal(go_sem, inc=1, device_id=(s, mirror), device_id_type=MESH)
        late_peers(send_min)

    @pl.when(c >= half)
    def _():
        pl.semaphore_wait(go_sem, 1)
        late_peers(send_min)

    wait_all(min_in, n_ctr - 1, recv_sems.at[0])
    near = near_ref[...] + 2.0 * jnp.min(min_in[...], axis=0)
    near_ref[...] = near
    cost = near * weight_ref[...]
    cost_out[...] = cost_code(cost)
    row_peers(lambda to: copy(cost_out, cost_in.at[s], 5, cost_sems.at[s], to).start(), True)
    cost_in[s] = cost_out[...]

    side = iota((LANES, LANES), 0) == iota((LANES, LANES), 1)
    own = assign_ref[pl.ds(c // 2, 1), :].astype(F32)
    own = jnp.sum(jnp.where(side, own, 0.0), axis=1, keepdims=True)
    own = jnp.where(c % 2 == 0, own[:n_own], own[n_own : 2 * n_own])
    first = (c * n_rows + s) * KO
    own = jnp.concatenate([own.astype(jnp.int32), first + iota((KO, 1), 0)], axis=0)
    own = jnp.broadcast_to(own, (n_own + KO, LANES))

    def add(r, values, sums):
        total, each = sums
        ids = wide_ids[r]
        for b in range(8):
            each = each + jnp.where(ids[b : b + 1, :] == own, values[b : b + 1, :], 0.0)
        return total + values, each

    zeros = (jnp.zeros((8, LANES), F32), jnp.zeros(own.shape, F32))

    def add_weight(r, sums):
        for h in range(2):
            wide_ids[r, 4 * h : 4 * h + 4] = ids_in[h, r, 0].astype(jnp.int32)
        return add(r, code_weight(jnp.concatenate([ids_in[0, r, 1], ids_in[1, r, 1]], axis=0)), sums)

    wait_all(ids_in.at[0], n_rows - 1, recv_sems.at[1])
    partner = (s + 1 - 2 * core, c)
    give = copy(ids_in.at[core], ids_in.at[core], 2, recv_sems.at[2], partner)
    give.start()
    give.wait_recv()
    weight_sum, size = lax.fori_loop(0, n_rows, add_weight, zeros)
    weight_sum = jnp.sum(weight_sum, keepdims=True)
    size = jnp.maximum(jnp.sum(size, axis=1, keepdims=True), 1.0)

    wait_all(label_in, n_rows - 1, recv_sems.at[3])
    for r in range(n_rows):
        labels[r : r + 1, :] = label_in[r]
    lane = iota((LANES, n_rows * KO), 1)
    at = iota((LANES, n_rows * KO), 0)
    place = (at == s * CAP + (lane & (CAP - 1))).astype(F32).astype(BF16)
    ids = dot_nn(labels[...].astype(BF16), place)
    slab = iota((n_rows, n_rows * KO), 0) == iota((n_rows, n_rows * KO), 1) // KO
    ids = jnp.sum(jnp.where(slab, ids, 0.0), axis=0, keepdims=True).astype(jnp.int32)
    at = iota((4 * KO, n_rows * KO), 0)
    quarter = (iota((4 * KO, n_rows * KO), 1) & (KO - 1)) >> 2
    member = ((at & (KO - 1)) == ids) & ((at >> 4) == quarter)
    member = member.astype(F32).astype(BF16)
    wait_all(rows_in, n_rows - 1, recv_sems.at[4])
    coord = dot_nn(member, rows_in[...].reshape(n_rows * KO, 256))
    for q in range(4):
        centroid_ref[:, q * 256 : (q + 1) * 256] = coord[q * KO : (q + 1) * KO, :] / size[n_own:]

    def add_cost(d, sums):
        r, _ = row_peer(d)
        pltpu.make_async_copy(cost_in.at[r], cost_in.at[r], cost_sems.at[r]).wait()
        return add(r, code_cost(cost_in[r]), sums)

    cost_sum, own_cost = lax.fori_loop(1, n_rows, add_cost, add(s, cost, zeros))
    mean = jnp.sum(cost_sum, keepdims=True) / weight_sum
    share = jnp.sum(own_cost, axis=1, keepdims=True) / (size * mean)
    diagonal = iota(own.shape, 0) == iota(own.shape, 1)
    share = jnp.sum(jnp.where(diagonal, share, 0.0), axis=0, keepdims=True)
    share_ref[...] = share[:, n_own : n_own + KO]
    near = near_ref[pl.ds(c // 2, 1), :]
    near = jnp.where(c % 2 == 0, near[:, :n_own], near[:, n_own : 2 * n_own])
    row_share_ref[...] = near / mean + 2.0 * share[:, :n_own]

    wait_all(min_in, n_ctr - 1, send_sems.at[0])
    wait_all(ids_in.at[0], n_rows - 1, send_sems.at[1])
    give.wait_send()
    wait_all(label_in, n_rows - 1, send_sems.at[3])
    wait_all(rows_in, n_rows - 1, send_sems.at[4])
    wait_all(cost_in, n_rows - 1, send_sems.at[5])


def deliver(*refs):
    n = len(refs) // 2
    for i in range(n):
        refs[n + i][...] = refs[i][...]


def local(points, centers, assignment, row_weight):
    slab_rows, width = points.shape
    block = centers.shape[0]
    n_rows = lax.axis_size("rows")
    n_ctr = lax.axis_size("ctr")
    vmem = pl.BlockSpec(memory_space=pltpu.VMEM)
    hbm = pl.BlockSpec(memory_space=pltpu.HBM)
    row_share, centroid, share = pl.pallas_call(
        functools.partial(kernel, n_rows, n_ctr),
        out_shape=(
            jax.ShapeDtypeStruct((1, slab_rows // n_ctr), F32),
            jax.ShapeDtypeStruct((KO, width), F32),
            jax.ShapeDtypeStruct((1, KO), F32),
        ),
        in_specs=[hbm, hbm, hbm, hbm],
        out_specs=(vmem, vmem, vmem),
        scratch_shapes=[
            pltpu.VMEM((slab_rows, width), BF16),
            pltpu.VMEM((block, width), BF16),
            pltpu.VMEM((8, LANES), jnp.int32),
            pltpu.VMEM((8, LANES), F32),
            pltpu.VMEM((3 * LANES, slab_rows), BF16),
            pltpu.VMEM((n_rows, 16, 256), BF16),
            pltpu.VMEM((n_rows, 16, 256), BF16),
            pltpu.VMEM((8, LANES), F32),
            pltpu.VMEM((n_ctr, 8, LANES), F32),
            pltpu.VMEM((2, 2, 4, LANES), CODE),
            pltpu.VMEM((2, n_rows, 2, 4, LANES), CODE),
            pltpu.VMEM((1, LANES), F32),
            pltpu.VMEM((n_rows, 1, LANES), F32),
            pltpu.VMEM((8, LANES), CODE),
            pltpu.VMEM((n_rows, 8, LANES), CODE),
            pltpu.VMEM((n_rows, 8, LANES), jnp.int32),
            pltpu.VMEM((n_rows, LANES), F32),
            pltpu.VMEM((8, LANES), F32),
            pltpu.SemaphoreType.DMA((7,)),
            pltpu.SemaphoreType.DMA((6,)),
            pltpu.SemaphoreType.DMA((5,)),
            pltpu.SemaphoreType.DMA((n_rows,)),
            pltpu.SemaphoreType.REGULAR,
            pltpu.SemaphoreType.REGULAR,
        ],
        compiler_params=pltpu.CompilerParams(
            collective_id=0, has_side_effects=True
        ),
        cost_estimate=pl.CostEstimate(
            flops=2 * slab_rows * width * (block + 3 * LANES),
            bytes_accessed=2 * (slab_rows + block) * width,
            transcendentals=0,
        ),
    )(points, centers, assignment.reshape(8, LANES), row_weight.reshape(8, LANES))
    made = (row_share, centroid, share)
    row_share, centroid, share = pl.pallas_call(
        deliver,
        out_shape=tuple(jax.ShapeDtypeStruct(x.shape, x.dtype) for x in made),
        in_specs=[vmem] * 3,
        out_specs=(vmem,) * 3,
    )(*made)
    return row_share.reshape(-1), centroid, share.reshape(-1)


def solution(mesh):
    placed = (P("rows", None), P("ctr", None), P("rows"), P("rows"))
    return jax.shard_map(
        local,
        mesh=mesh,
        in_specs=placed,
        out_specs=(P(("rows", "ctr")), P(("ctr", "rows"), None), P(("ctr", "rows"))),
        check_vma=False,
    )
```

```python
import functools

import jax
import jax.numpy as jnp
from jax import lax
from jax.experimental import pallas as pl
from jax.experimental.pallas import tpu as pltpu
from jax.sharding import PartitionSpec as P

KO = 16
CAP = 4
LANES = 128
MESH = pl.DeviceIdType.MESH
F32 = jnp.float32
BF16 = jnp.bfloat16
CODE = jnp.int16


def iota(shape, dim):
    return lax.broadcasted_iota(jnp.int32, shape, dim)


def dot_nt(a, b):
    return lax.dot_general(a, b, (((1,), (1,)), ((), ())), preferred_element_type=F32)


def dot_nn(a, b):
    return lax.dot_general(a, b, (((1,), (0,)), ((), ())), preferred_element_type=F32)


def split3(x):
    hi = x.astype(BF16).astype(F32)
    mid = (x - hi).astype(BF16).astype(F32)
    lo = ((x - hi) - mid).astype(BF16).astype(F32)
    return [hi, mid, lo]


def weight_code(x):
    return (((x - 0.25) * (65535 / 3.75) + 0.5).astype(jnp.int32) - 32768).astype(CODE)


def code_weight(code):
    return (code.astype(jnp.int32) + 32768).astype(F32) * (3.75 / 65535) + 0.25


def cost_code(x):
    at = (jnp.log2(jnp.maximum(x, 2.0**-106)) + 106.0) * 512.0 + 0.5
    return (jnp.minimum(at, 65535.0).astype(jnp.int32) - 32768).astype(CODE)


def code_cost(code):
    return jnp.exp2((code.astype(jnp.int32) + 32768).astype(F32) * (1 / 512) - 106.0)


def spread(parts):
    stack = jnp.concatenate(parts, axis=0)
    block = iota(stack.shape, 0) & 7
    return jnp.concatenate([jnp.where(block == b, stack, 0.0) for b in range(8)], axis=1).astype(BF16)


def kernel(
    n_rows,
    n_ctr,
    points_hbm,
    centers_hbm,
    assign_hbm,
    weight_hbm,
    row_share_ref,
    centroid_ref,
    share_ref,
    points,
    centers,
    assign_ref,
    weight_ref,
    pick,
    rows_out,
    rows_in,
    min_out,
    min_in,
    ids_out,
    ids_in,
    label_out,
    label_in,
    cost_out,
    cost_in,
    wide_ids,
    labels,
    near_ref,
    load_sem,
    send_sems,
    recv_sems,
    cost_sems,
    late_sem,
    go_sem,
):
    s = lax.axis_index("rows")
    c = lax.axis_index("ctr")
    chunk = points.shape[0] // 4
    n_own = row_share_ref.shape[1]

    def row_peer(d):
        k = d >> 2
        away = ((k + 1) >> 1) * (2 * (k & 1) - 1)
        low = (s + d) & 3
        r = (((s >> 2) + away) & (n_rows // 4 - 1)) * 4 + low
        other = ((low >> 1) + (s >> 1)) & 1
        return r, c + other * (1 - 2 * (c & 1))

    def row_peers(act, unroll=False):
        if unroll:
            for d in range(n_rows - 1, 0, -1):
                act(row_peer(d))
            return

        def step(d, carry):
            act(row_peer(n_rows - d))
            return carry

        lax.fori_loop(1, n_rows, step, 0)

    half = n_ctr // 2

    def early_peers(act):
        for d in sorted(range(half), key=lambda d: abs(2 * d - half)):
            p = (c + d) & (half - 1)
            pl.when(p != c)(functools.partial(act, p))

    def late_peers(act):
        for d in range(half):
            p = half + ((c + d) & (half - 1))
            pl.when(p != c)(functools.partial(act, p))

    barrier = pltpu.get_barrier_semaphore()
    assign_load = pltpu.make_async_copy(assign_hbm, assign_ref, load_sem.at[5])
    assign_load.start()
    weight_load = pltpu.make_async_copy(weight_hbm, weight_ref, load_sem.at[6])
    weight_load.start()

    center_load = pltpu.make_async_copy(centers_hbm, centers, load_sem.at[4])
    center_load.start()
    point_loads = []
    for q in range(4):
        part = pl.ds(q * chunk, chunk)
        load = pltpu.make_async_copy(points_hbm.at[part], points.at[part], load_sem.at[q])
        load.start()
        point_loads.append(load)

    def enter(p):
        pl.semaphore_signal(barrier, inc=1, device_id=(s, p), device_id_type=MESH)

    @pl.when(c < half)
    def _():
        early_peers(enter)
        late_peers(enter)

    row_peers(lambda to: pl.semaphore_signal(barrier, inc=1, device_id=to, device_id_type=MESH), True)

    def slots():
        assign = assign_ref[...]
        weight = weight_ref[...]
        for h in range(2):
            ids_out[h, 0] = assign[4 * h : 4 * h + 4].astype(CODE)
            ids_out[h, 1] = weight_code(weight[4 * h : 4 * h + 4])
        run = (assign >> 4) & (n_rows - 1)
        other = ((run >> 1) + lax.rem(s, 4) // 2) & 1
        run = jnp.where(assign >> 9 == c + other * (1 - 2 * lax.rem(c, 2)), run, -1)
        member = (assign & (KO - 1)).astype(F32)
        hot = [(run[b : b + 1, :] == iota((n_rows, LANES), 0)).astype(F32) for b in range(8)]
        before = jnp.concatenate(
            [
                (iota((LANES, LANES), 0) < iota((LANES, LANES), 1)).astype(F32),
                jnp.ones((LANES, LANES), F32),
            ],
            axis=1,
        ).astype(BF16)
        counted = dot_nn(jnp.concatenate(hot, axis=0).astype(BF16), before)
        carry = jnp.zeros((n_rows, LANES), F32)
        for b in range(8):
            rank = counted[b * n_rows : (b + 1) * n_rows, :LANES] + carry
            carry = carry + counted[b * n_rows : (b + 1) * n_rows, LANES:]
            rank = jnp.sum(hot[b] * rank, axis=0, keepdims=True).astype(jnp.int32)
            here = run[b : b + 1, :]
            code = jnp.where(here >= 0, here * CAP + rank, -1)
            lanes = pl.ds(b * LANES, LANES)
            pick[0:LANES, lanes] = (iota((LANES, LANES), 0) == code).astype(F32).astype(BF16)
            at = iota((2 * LANES, LANES), 0)
            at = (at >> 3) * CAP + (at & (CAP - 1))
            pick[LANES : 3 * LANES, lanes] = (at == code).astype(F32).astype(BF16)

        traits = spread([member + 1.0] + split3(weight))
        label_out[...] = jnp.sum(dot_nt(traits[0:8], pick[0:LANES, :]), axis=0, keepdims=True) - 1.0

        row_weight = jnp.sum(dot_nt(pick[LANES : 3 * LANES, :], traits[8:32]), axis=1, keepdims=True)
        odd = (iota((2 * LANES, 256), 0) >> 2) & 1
        tiles = []
        for t in range(2):
            low = dot_nn(pick[LANES : 3 * LANES, :], points[:, pl.ds(2 * t * 256, 256)])
            high = dot_nn(pick[LANES : 3 * LANES, :], points[:, pl.ds((2 * t + 1) * 256, 256)])
            tiles.append((jnp.where(odd == 0, low, high) * row_weight).reshape(n_rows, 8, 256))
        rows_out[...] = jnp.concatenate(tiles, axis=1).astype(BF16)

    assign_load.wait()
    weight_load.wait()
    def loaded(first, last):
        for load in point_loads[first:last]:
            load.wait()

    @pl.when(c < half)
    def _():
        loaded(0, 4)
        slots()

    pl.when(c >= half)(functools.partial(loaded, 0, 2))

    center_load.wait()
    wide = centers[...].astype(F32)
    half_norm = 0.5 * jnp.sum(wide * wide, axis=1, keepdims=True)
    for q in range(4):
        if q == 2:
            pl.when(c >= half)(functools.partial(loaded, 2, 4))
        some = points[q * chunk : (q + 1) * chunk, :]
        least = jnp.min(half_norm - dot_nt(centers[...], some), axis=0, keepdims=True)
        for k in range(2):
            min_out[2 * q + k : 2 * q + k + 1, :] = least[:, k * LANES : (k + 1) * LANES]

    pl.semaphore_wait(barrier, n_rows + half - 2 + c // half)

    def copy(src, dst, i, recv, device):
        return pltpu.make_async_remote_copy(
            src, dst, send_sems.at[i], recv, device_id=device, device_id_type=MESH
        )

    def wait_all(ref, count, sem):
        whole = ref.at[pl.ds(0, count)]
        pltpu.make_async_copy(whole, whole, sem).wait()

    def send_min(p):
        copy(min_out, min_in.at[c], 0, recv_sems.at[0], (s, p)).start()

    def tell_late(p):
        pl.semaphore_signal(late_sem, inc=1, device_id=(s, p), device_id_type=MESH)

    early_peers(send_min)

    @pl.when(c >= half)
    def _():
        early_peers(tell_late)
        slots()

    for q in range(4):
        wide = points[q * chunk : (q + 1) * chunk, :].astype(F32)
        wide = wide * wide
        total = wide[:, 0:LANES]
        for k in range(1, 8):
            total = total + wide[:, k * LANES : (k + 1) * LANES]
        norm = jnp.sum(total.T, axis=0, keepdims=True)
        for k in range(2):
            near_ref[2 * q + k : 2 * q + k + 1, :] = norm[:, k * LANES : (k + 1) * LANES]

    def send_half(src, dst, i):
        def send(to):
            h = to[0] & 1
            copy(src.at[h], dst.at[h, s], i, recv_sems.at[i], to).start()

        row_peers(send)

    core = s & 1
    send_half(ids_out, ids_in, 1)
    row_peers(lambda to: copy(label_out, label_in.at[s], 3, recv_sems.at[3], to).start())
    row_peers(lambda to: copy(rows_out.at[to[0]], rows_in.at[s], 4, recv_sems.at[4], to).start())
    min_in[c] = min_out[...]
    ids_in[core, s] = ids_out[core]
    label_in[s] = label_out[...]
    rows_in[s] = rows_out[s]

    @pl.when(c < half)
    def _():
        pl.semaphore_wait(late_sem, half)
        mirror = n_ctr - 2 - 2 * (c // 2) + c % 2
        pl.semaphore_signal(go_sem, inc=1, device_id=(s, mirror), device_id_type=MESH)
        late_peers(send_min)

    @pl.when(c >= half)
    def _():
        pl.semaphore_wait(go_sem, 1)
        late_peers(send_min)

    wait_all(min_in, n_ctr - 1, recv_sems.at[0])
    near = near_ref[...] + 2.0 * jnp.min(min_in[...], axis=0)
    near_ref[...] = near
    cost = near * weight_ref[...]
    cost_out[...] = cost_code(cost)
    row_peers(lambda to: copy(cost_out, cost_in.at[s], 5, cost_sems.at[s], to).start(), True)
    cost_in[s] = cost_out[...]

    side = iota((LANES, LANES), 0) == iota((LANES, LANES), 1)
    own = assign_ref[pl.ds(c // 2, 1), :].astype(F32)
    own = jnp.sum(jnp.where(side, own, 0.0), axis=1, keepdims=True)
    own = jnp.where(c % 2 == 0, own[:n_own], own[n_own : 2 * n_own])
    first = (c * n_rows + s) * KO
    own = jnp.concatenate([own.astype(jnp.int32), first + iota((KO, 1), 0)], axis=0)
    own = jnp.broadcast_to(own, (n_own + KO, LANES))

    def add(r, values, sums):
        total, each = sums
        ids = wide_ids[r]
        for b in range(8):
            each = each + jnp.where(ids[b : b + 1, :] == own, values[b : b + 1, :], 0.0)
        return total + values, each

    zeros = (jnp.zeros((8, LANES), F32), jnp.zeros(own.shape, F32))

    def add_weight(r, sums):
        for h in range(2):
            wide_ids[r, 4 * h : 4 * h + 4] = ids_in[h, r, 0].astype(jnp.int32)
        return add(r, code_weight(jnp.concatenate([ids_in[0, r, 1], ids_in[1, r, 1]], axis=0)), sums)

    wait_all(ids_in.at[0], n_rows - 1, recv_sems.at[1])
    partner = (s + 1 - 2 * core, c)
    give = copy(ids_in.at[core], ids_in.at[core], 2, recv_sems.at[2], partner)
    give.start()
    give.wait_recv()
    weight_sum, size = lax.fori_loop(0, n_rows, add_weight, zeros)
    weight_sum = jnp.sum(weight_sum, keepdims=True)
    size = jnp.maximum(jnp.sum(size, axis=1, keepdims=True), 1.0)

    wait_all(label_in, n_rows - 1, recv_sems.at[3])
    for r in range(n_rows):
        labels[r : r + 1, :] = label_in[r]
    lane = iota((LANES, n_rows * KO), 1)
    at = iota((LANES, n_rows * KO), 0)
    place = (at == s * CAP + (lane & (CAP - 1))).astype(F32).astype(BF16)
    ids = dot_nn(labels[...].astype(BF16), place)
    slab = iota((n_rows, n_rows * KO), 0) == iota((n_rows, n_rows * KO), 1) // KO
    ids = jnp.sum(jnp.where(slab, ids, 0.0), axis=0, keepdims=True).astype(jnp.int32)
    at = iota((4 * KO, n_rows * KO), 0)
    quarter = (iota((4 * KO, n_rows * KO), 1) & (KO - 1)) >> 2
    member = ((at & (KO - 1)) == ids) & ((at >> 4) == quarter)
    member = member.astype(F32).astype(BF16)
    wait_all(rows_in, n_rows - 1, recv_sems.at[4])
    coord = dot_nn(member, rows_in[...].reshape(n_rows * KO, 256))
    for q in range(4):
        centroid_ref[:, q * 256 : (q + 1) * 256] = coord[q * KO : (q + 1) * KO, :] / size[n_own:]

    def add_cost(d, sums):
        r, _ = row_peer(d)
        pltpu.make_async_copy(cost_in.at[r], cost_in.at[r], cost_sems.at[r]).wait()
        return add(r, code_cost(cost_in[r]), sums)

    cost_sum, own_cost = lax.fori_loop(1, n_rows, add_cost, add(s, cost, zeros))
    mean = jnp.sum(cost_sum, keepdims=True) / weight_sum
    share = jnp.sum(own_cost, axis=1, keepdims=True) / (size * mean)
    diagonal = iota(own.shape, 0) == iota(own.shape, 1)
    share = jnp.sum(jnp.where(diagonal, share, 0.0), axis=0, keepdims=True)
    share_ref[...] = share[:, n_own : n_own + KO]
    near = near_ref[pl.ds(c // 2, 1), :]
    near = jnp.where(c % 2 == 0, near[:, :n_own], near[:, n_own : 2 * n_own])
    row_share_ref[...] = near / mean + 2.0 * share[:, :n_own]

    wait_all(min_in, n_ctr - 1, send_sems.at[0])
    wait_all(ids_in.at[0], n_rows - 1, send_sems.at[1])
    give.wait_send()
    wait_all(label_in, n_rows - 1, send_sems.at[3])
    wait_all(rows_in, n_rows - 1, send_sems.at[4])
    wait_all(cost_in, n_rows - 1, send_sems.at[5])


def deliver(*refs):
    n = len(refs) // 2
    for i in range(n):
        refs[n + i][...] = refs[i][...]


def local(points, centers, assignment, row_weight):
    slab_rows, width = points.shape
    block = centers.shape[0]
    n_rows = lax.axis_size("rows")
    n_ctr = lax.axis_size("ctr")
    vmem = pl.BlockSpec(memory_space=pltpu.VMEM)
    hbm = pl.BlockSpec(memory_space=pltpu.HBM)
    row_share, centroid, share = pl.pallas_call(
        functools.partial(kernel, n_rows, n_ctr),
        out_shape=(
            pltpu.VMEM((1, slab_rows // n_ctr), F32),
            pltpu.VMEM((KO, width), F32),
            pltpu.VMEM((1, KO), F32),
        ),
        in_specs=[hbm, hbm, hbm, hbm],
        out_specs=(vmem, vmem, vmem),
        scratch_shapes=[
            pltpu.VMEM((slab_rows, width), BF16),
            pltpu.VMEM((block, width), BF16),
            pltpu.VMEM((8, LANES), jnp.int32),
            pltpu.VMEM((8, LANES), F32),
            pltpu.VMEM((3 * LANES, slab_rows), BF16),
            pltpu.VMEM((n_rows, 16, 256), BF16),
            pltpu.VMEM((n_rows, 16, 256), BF16),
            pltpu.VMEM((8, LANES), F32),
            pltpu.VMEM((n_ctr, 8, LANES), F32),
            pltpu.VMEM((2, 2, 4, LANES), CODE),
            pltpu.VMEM((2, n_rows, 2, 4, LANES), CODE),
            pltpu.VMEM((1, LANES), F32),
            pltpu.VMEM((n_rows, 1, LANES), F32),
            pltpu.VMEM((8, LANES), CODE),
            pltpu.VMEM((n_rows, 8, LANES), CODE),
            pltpu.VMEM((n_rows, 8, LANES), jnp.int32),
            pltpu.VMEM((n_rows, LANES), F32),
            pltpu.VMEM((8, LANES), F32),
            pltpu.SemaphoreType.DMA((7,)),
            pltpu.SemaphoreType.DMA((6,)),
            pltpu.SemaphoreType.DMA((5,)),
            pltpu.SemaphoreType.DMA((n_rows,)),
            pltpu.SemaphoreType.REGULAR,
            pltpu.SemaphoreType.REGULAR,
        ],
        compiler_params=pltpu.CompilerParams(
            collective_id=0, has_side_effects=True, vmem_limit_bytes=48 * 1024 * 1024
        ),
        cost_estimate=pl.CostEstimate(
            flops=2 * slab_rows * width * (block + 3 * LANES),
            bytes_accessed=2 * (slab_rows + block) * width,
            transcendentals=0,
        ),
    )(*(pltpu.with_memory_space_constraint(x, pltpu.HBM) for x in (points, centers, assignment.reshape(8, LANES), row_weight.reshape(8, LANES))))
    made = (row_share, centroid, share)
    row_share, centroid, share = pl.pallas_call(
        deliver,
        out_shape=tuple(jax.ShapeDtypeStruct(x.shape, x.dtype) for x in made),
        in_specs=[vmem] * 3,
        out_specs=(vmem,) * 3,
        compiler_params=pltpu.CompilerParams(vmem_limit_bytes=4 * 1024 * 1024),
    )(*made)
    return row_share.reshape(-1), centroid, share.reshape(-1)


def solution(mesh):
    placed = (P("rows", None), P("ctr", None), P("rows"), P("rows"))
    return jax.shard_map(
        local,
        mesh=mesh,
        in_specs=placed,
        out_specs=(P(("rows", "ctr")), P(("ctr", "rows"), None), P(("ctr", "rows"))),
        check_vma=False,
    )
```

```python
import functools

import jax
import jax.numpy as jnp
from jax import lax
from jax.experimental import pallas as pl
from jax.experimental.pallas import tpu as pltpu
from jax.sharding import PartitionSpec as P

KO = 16
CAP = 4
LANES = 128
MESH = pl.DeviceIdType.MESH
F32 = jnp.float32
BF16 = jnp.bfloat16
CODE = jnp.int16


def iota(shape, dim):
    return lax.broadcasted_iota(jnp.int32, shape, dim)


def dot_nt(a, b):
    return lax.dot_general(a, b, (((1,), (1,)), ((), ())), preferred_element_type=F32)


def dot_nn(a, b):
    return lax.dot_general(a, b, (((1,), (0,)), ((), ())), preferred_element_type=F32)


def split3(x):
    hi = x.astype(BF16).astype(F32)
    mid = (x - hi).astype(BF16).astype(F32)
    lo = ((x - hi) - mid).astype(BF16).astype(F32)
    return [hi, mid, lo]


def weight_code(x):
    return (((x - 0.25) * (65535 / 3.75) + 0.5).astype(jnp.int32) - 32768).astype(CODE)


def code_weight(code):
    return (code.astype(jnp.int32) + 32768).astype(F32) * (3.75 / 65535) + 0.25


def cost_code(x):
    at = (jnp.log2(jnp.maximum(x, 2.0**-106)) + 106.0) * 512.0 + 0.5
    return (jnp.minimum(at, 65535.0).astype(jnp.int32) - 32768).astype(CODE)


def code_cost(code):
    return jnp.exp2((code.astype(jnp.int32) + 32768).astype(F32) * (1 / 512) - 106.0)


def spread(parts):
    stack = jnp.concatenate(parts, axis=0)
    block = iota(stack.shape, 0) & 7
    return jnp.concatenate([jnp.where(block == b, stack, 0.0) for b in range(8)], axis=1).astype(BF16)


def kernel(
    n_rows,
    n_ctr,
    points_hbm,
    centers_hbm,
    assign_hbm,
    weight_hbm,
    row_share_ref,
    centroid_ref,
    share_ref,
    points,
    centers,
    assign_ref,
    weight_ref,
    pick,
    rows_out,
    rows_in,
    min_out,
    min_in,
    ids_out,
    ids_in,
    label_out,
    label_in,
    cost_out,
    cost_in,
    wide_ids,
    labels,
    near_ref,
    load_sem,
    send_sems,
    recv_sems,
    cost_sems,
    late_sem,
    go_sem,
):
    s = lax.axis_index("rows")
    c = lax.axis_index("ctr")
    chunk = points.shape[0] // 4
    n_own = row_share_ref.shape[1]

    def row_peer(d):
        k = d >> 2
        away = ((k + 1) >> 1) * (2 * (k & 1) - 1)
        low = (s + d) & 3
        r = (((s >> 2) + away) & (n_rows // 4 - 1)) * 4 + low
        other = ((low >> 1) + (s >> 1)) & 1
        return r, c + other * (1 - 2 * (c & 1))

    def row_peers(act, unroll=False):
        if unroll:
            for d in range(n_rows - 1, 0, -1):
                act(row_peer(d))
            return

        def step(d, carry):
            act(row_peer(n_rows - d))
            return carry

        lax.fori_loop(1, n_rows, step, 0)

    half = n_ctr // 2

    def early_peers(act):
        for p in range(half):
            pl.when(p != c)(functools.partial(act, p))

    def late_peers(act):
        for p in range(half, n_ctr):
            pl.when(p != c)(functools.partial(act, p))

    barrier = pltpu.get_barrier_semaphore()
    center_load = pltpu.make_async_copy(centers_hbm, centers, load_sem.at[4])
    center_load.start()
    point_loads = []
    for q in range(4):
        part = pl.ds(q * chunk, chunk)
        load = pltpu.make_async_copy(points_hbm.at[part], points.at[part], load_sem.at[q])
        load.start()
        point_loads.append(load)
    assign_load = pltpu.make_async_copy(assign_hbm, assign_ref, load_sem.at[5])
    assign_load.start()
    weight_load = pltpu.make_async_copy(weight_hbm, weight_ref, load_sem.at[6])
    weight_load.start()

    def enter(p):
        pl.semaphore_signal(barrier, inc=1, device_id=(s, p), device_id_type=MESH)

    @pl.when(c < half)
    def _():
        early_peers(enter)
        late_peers(enter)

    row_peers(lambda to: pl.semaphore_signal(barrier, inc=1, device_id=to, device_id_type=MESH), True)

    def slots():
        assign = assign_ref[...]
        weight = weight_ref[...]
        for h in range(2):
            ids_out[h, 0] = assign[4 * h : 4 * h + 4].astype(CODE)
            ids_out[h, 1] = weight_code(weight[4 * h : 4 * h + 4])
        run = (assign >> 4) & (n_rows - 1)
        other = ((run >> 1) + lax.rem(s, 4) // 2) & 1
        run = jnp.where(assign >> 9 == c + other * (1 - 2 * lax.rem(c, 2)), run, -1)
        member = (assign & (KO - 1)).astype(F32)
        hot = [(run[b : b + 1, :] == iota((n_rows, LANES), 0)).astype(F32) for b in range(8)]
        before = jnp.concatenate(
            [
                (iota((LANES, LANES), 0) < iota((LANES, LANES), 1)).astype(F32),
                jnp.ones((LANES, LANES), F32),
            ],
            axis=1,
        ).astype(BF16)
        counted = dot_nn(jnp.concatenate(hot, axis=0).astype(BF16), before)
        carry = jnp.zeros((n_rows, LANES), F32)
        for b in range(8):
            rank = counted[b * n_rows : (b + 1) * n_rows, :LANES] + carry
            carry = carry + counted[b * n_rows : (b + 1) * n_rows, LANES:]
            rank = jnp.sum(hot[b] * rank, axis=0, keepdims=True).astype(jnp.int32)
            here = run[b : b + 1, :]
            code = jnp.where(here >= 0, here * CAP + rank, -1)
            lanes = pl.ds(b * LANES, LANES)
            pick[0:LANES, lanes] = (iota((LANES, LANES), 0) == code).astype(F32).astype(BF16)
            at = iota((2 * LANES, LANES), 0)
            at = (at >> 3) * CAP + (at & (CAP - 1))
            pick[LANES : 3 * LANES, lanes] = (at == code).astype(F32).astype(BF16)

        traits = spread([member + 1.0] + split3(weight))
        label_out[...] = jnp.sum(dot_nt(traits[0:8], pick[0:LANES, :]), axis=0, keepdims=True) - 1.0

        row_weight = jnp.sum(dot_nt(pick[LANES : 3 * LANES, :], traits[8:32]), axis=1, keepdims=True)
        odd = (iota((2 * LANES, 256), 0) >> 2) & 1
        tiles = []
        for t in range(2):
            low = dot_nn(pick[LANES : 3 * LANES, :], points[:, pl.ds(2 * t * 256, 256)])
            high = dot_nn(pick[LANES : 3 * LANES, :], points[:, pl.ds((2 * t + 1) * 256, 256)])
            tiles.append((jnp.where(odd == 0, low, high) * row_weight).reshape(n_rows, 8, 256))
        rows_out[...] = jnp.concatenate(tiles, axis=1).astype(BF16)

    assign_load.wait()
    weight_load.wait()
    def loaded(first, last):
        for load in point_loads[first:last]:
            load.wait()

    @pl.when(c < half)
    def _():
        loaded(0, 4)
        slots()

    pl.when(c >= half)(functools.partial(loaded, 0, 2))

    center_load.wait()
    wide = centers[...].astype(F32)
    half_norm = 0.5 * jnp.sum(wide * wide, axis=1, keepdims=True)
    for q in range(4):
        if q == 2:
            pl.when(c >= half)(functools.partial(loaded, 2, 4))
        some = points[q * chunk : (q + 1) * chunk, :]
        least = jnp.min(half_norm - dot_nt(centers[...], some), axis=0, keepdims=True)
        for k in range(2):
            min_out[2 * q + k : 2 * q + k + 1, :] = least[:, k * LANES : (k + 1) * LANES]

    pl.semaphore_wait(barrier, n_rows + half - 2 + c // half)

    def copy(src, dst, i, recv, device):
        return pltpu.make_async_remote_copy(
            src, dst, send_sems.at[i], recv, device_id=device, device_id_type=MESH
        )

    def wait_all(ref, count, sem):
        whole = ref.at[pl.ds(0, count)]
        pltpu.make_async_copy(whole, whole, sem).wait()

    def send_min(p):
        copy(min_out, min_in.at[c], 0, recv_sems.at[0], (s, p)).start()

    def tell_late(p):
        pl.semaphore_signal(late_sem, inc=1, device_id=(s, p), device_id_type=MESH)

    early_peers(send_min)

    @pl.when(c >= half)
    def _():
        early_peers(tell_late)
        slots()

    for q in range(4):
        wide = points[q * chunk : (q + 1) * chunk, :].astype(F32)
        wide = wide * wide
        total = wide[:, 0:LANES]
        for k in range(1, 8):
            total = total + wide[:, k * LANES : (k + 1) * LANES]
        norm = jnp.sum(total.T, axis=0, keepdims=True)
        for k in range(2):
            near_ref[2 * q + k : 2 * q + k + 1, :] = norm[:, k * LANES : (k + 1) * LANES]

    def send_half(src, dst, i):
        def send(to):
            h = to[0] & 1
            copy(src.at[h], dst.at[h, s], i, recv_sems.at[i], to).start()

        row_peers(send)

    core = s & 1
    send_half(ids_out, ids_in, 1)
    row_peers(lambda to: copy(label_out, label_in.at[s], 3, recv_sems.at[3], to).start())
    row_peers(lambda to: copy(rows_out.at[to[0]], rows_in.at[s], 4, recv_sems.at[4], to).start())
    min_in[c] = min_out[...]
    ids_in[core, s] = ids_out[core]
    label_in[s] = label_out[...]
    rows_in[s] = rows_out[s]

    @pl.when(c < half)
    def _():
        pl.semaphore_wait(late_sem, half)
        mirror = n_ctr - 2 - 2 * (c // 2) + c % 2
        pl.semaphore_signal(go_sem, inc=1, device_id=(s, mirror), device_id_type=MESH)
        late_peers(send_min)

    @pl.when(c >= half)
    def _():
        pl.semaphore_wait(go_sem, 1)
        late_peers(send_min)

    wait_all(min_in, n_ctr - 1, recv_sems.at[0])
    near = near_ref[...] + 2.0 * jnp.min(min_in[...], axis=0)
    near_ref[...] = near
    cost = near * weight_ref[...]
    cost_out[...] = cost_code(cost)
    row_peers(lambda to: copy(cost_out, cost_in.at[s], 5, cost_sems.at[s], to).start(), True)
    cost_in[s] = cost_out[...]

    side = iota((LANES, LANES), 0) == iota((LANES, LANES), 1)
    own = assign_ref[pl.ds(c // 2, 1), :].astype(F32)
    own = jnp.sum(jnp.where(side, own, 0.0), axis=1, keepdims=True)
    own = jnp.where(c % 2 == 0, own[:n_own], own[n_own : 2 * n_own])
    first = (c * n_rows + s) * KO
    own = jnp.concatenate([own.astype(jnp.int32), first + iota((KO, 1), 0)], axis=0)
    own = jnp.broadcast_to(own, (n_own + KO, LANES))

    def add(r, values, sums):
        total, each = sums
        ids = wide_ids[r]
        for b in range(8):
            each = each + jnp.where(ids[b : b + 1, :] == own, values[b : b + 1, :], 0.0)
        return total + values, each

    zeros = (jnp.zeros((8, LANES), F32), jnp.zeros(own.shape, F32))

    def add_weight(r, sums):
        for h in range(2):
            wide_ids[r, 4 * h : 4 * h + 4] = ids_in[h, r, 0].astype(jnp.int32)
        return add(r, code_weight(jnp.concatenate([ids_in[0, r, 1], ids_in[1, r, 1]], axis=0)), sums)

    wait_all(ids_in.at[0], n_rows - 1, recv_sems.at[1])
    partner = (s + 1 - 2 * core, c)
    give = copy(ids_in.at[core], ids_in.at[core], 2, recv_sems.at[2], partner)
    give.start()
    give.wait_recv()
    weight_sum, size = lax.fori_loop(0, n_rows, add_weight, zeros)
    weight_sum = jnp.sum(weight_sum, keepdims=True)
    size = jnp.maximum(jnp.sum(size, axis=1, keepdims=True), 1.0)

    wait_all(label_in, n_rows - 1, recv_sems.at[3])
    for r in range(n_rows):
        labels[r : r + 1, :] = label_in[r]
    lane = iota((LANES, n_rows * KO), 1)
    at = iota((LANES, n_rows * KO), 0)
    place = (at == s * CAP + (lane & (CAP - 1))).astype(F32).astype(BF16)
    ids = dot_nn(labels[...].astype(BF16), place)
    slab = iota((n_rows, n_rows * KO), 0) == iota((n_rows, n_rows * KO), 1) // KO
    ids = jnp.sum(jnp.where(slab, ids, 0.0), axis=0, keepdims=True).astype(jnp.int32)
    at = iota((4 * KO, n_rows * KO), 0)
    quarter = (iota((4 * KO, n_rows * KO), 1) & (KO - 1)) >> 2
    member = ((at & (KO - 1)) == ids) & ((at >> 4) == quarter)
    member = member.astype(F32).astype(BF16)
    wait_all(rows_in, n_rows - 1, recv_sems.at[4])
    coord = dot_nn(member, rows_in[...].reshape(n_rows * KO, 256))
    for q in range(4):
        centroid_ref[:, q * 256 : (q + 1) * 256] = coord[q * KO : (q + 1) * KO, :] / size[n_own:]

    def add_costs(first, count, sums):
        slabs = [row_peer(first + j)[0] for j in range(count)]
        for r in slabs:
            pltpu.make_async_copy(cost_in.at[r], cost_in.at[r], cost_sems.at[r]).wait()
        for r in slabs:
            sums = add(r, code_cost(cost_in[r]), sums)
        return sums

    sums = add_costs(1, 3, add(s, cost, zeros))
    cost_sum, own_cost = lax.fori_loop(1, n_rows // 4, lambda k, sums: add_costs(4 * k, 4, sums), sums)
    mean = jnp.sum(cost_sum, keepdims=True) / weight_sum
    share = jnp.sum(own_cost, axis=1, keepdims=True) / (size * mean)
    diagonal = iota(own.shape, 0) == iota(own.shape, 1)
    share = jnp.sum(jnp.where(diagonal, share, 0.0), axis=0, keepdims=True)
    share_ref[...] = share[:, n_own : n_own + KO]
    near = near_ref[pl.ds(c // 2, 1), :]
    near = jnp.where(c % 2 == 0, near[:, :n_own], near[:, n_own : 2 * n_own])
    row_share_ref[...] = near / mean + 2.0 * share[:, :n_own]

    wait_all(min_in, n_ctr - 1, send_sems.at[0])
    wait_all(ids_in.at[0], n_rows - 1, send_sems.at[1])
    give.wait_send()
    wait_all(label_in, n_rows - 1, send_sems.at[3])
    wait_all(rows_in, n_rows - 1, send_sems.at[4])
    wait_all(cost_in, n_rows - 1, send_sems.at[5])


def deliver(*refs):
    n = len(refs) // 2
    for i in range(n):
        refs[n + i][...] = refs[i][...]


def local(points, centers, assignment, row_weight):
    slab_rows, width = points.shape
    block = centers.shape[0]
    n_rows = lax.axis_size("rows")
    n_ctr = lax.axis_size("ctr")
    vmem = pl.BlockSpec(memory_space=pltpu.VMEM)
    hbm = pl.BlockSpec(memory_space=pltpu.HBM)
    row_share, centroid, share = pl.pallas_call(
        functools.partial(kernel, n_rows, n_ctr),
        out_shape=(
            pltpu.VMEM((1, slab_rows // n_ctr), F32),
            pltpu.VMEM((KO, width), F32),
            pltpu.VMEM((1, KO), F32),
        ),
        in_specs=[hbm, hbm, hbm, hbm],
        out_specs=(vmem, vmem, vmem),
        scratch_shapes=[
            pltpu.VMEM((slab_rows, width), BF16),
            pltpu.VMEM((block, width), BF16),
            pltpu.VMEM((8, LANES), jnp.int32),
            pltpu.VMEM((8, LANES), F32),
            pltpu.VMEM((3 * LANES, slab_rows), BF16),
            pltpu.VMEM((n_rows, 16, 256), BF16),
            pltpu.VMEM((n_rows, 16, 256), BF16),
            pltpu.VMEM((8, LANES), F32),
            pltpu.VMEM((n_ctr, 8, LANES), F32),
            pltpu.VMEM((2, 2, 4, LANES), CODE),
            pltpu.VMEM((2, n_rows, 2, 4, LANES), CODE),
            pltpu.VMEM((1, LANES), F32),
            pltpu.VMEM((n_rows, 1, LANES), F32),
            pltpu.VMEM((8, LANES), CODE),
            pltpu.VMEM((n_rows, 8, LANES), CODE),
            pltpu.VMEM((n_rows, 8, LANES), jnp.int32),
            pltpu.VMEM((n_rows, LANES), F32),
            pltpu.VMEM((8, LANES), F32),
            pltpu.SemaphoreType.DMA((7,)),
            pltpu.SemaphoreType.DMA((6,)),
            pltpu.SemaphoreType.DMA((5,)),
            pltpu.SemaphoreType.DMA((n_rows,)),
            pltpu.SemaphoreType.REGULAR,
            pltpu.SemaphoreType.REGULAR,
        ],
        compiler_params=pltpu.CompilerParams(
            collective_id=0, has_side_effects=True, vmem_limit_bytes=48 * 1024 * 1024
        ),
        cost_estimate=pl.CostEstimate(
            flops=2 * slab_rows * width * (block + 3 * LANES),
            bytes_accessed=2 * (slab_rows + block) * width,
            transcendentals=0,
        ),
    )(*(pltpu.with_memory_space_constraint(x, pltpu.HBM) for x in (points, centers, assignment.reshape(8, LANES), row_weight.reshape(8, LANES))))
    made = (row_share, centroid, share)
    row_share, centroid, share = pl.pallas_call(
        deliver,
        out_shape=tuple(jax.ShapeDtypeStruct(x.shape, x.dtype) for x in made),
        in_specs=[vmem] * 3,
        out_specs=(vmem,) * 3,
        compiler_params=pltpu.CompilerParams(vmem_limit_bytes=4 * 1024 * 1024),
    )(*made)
    return row_share.reshape(-1), centroid, share.reshape(-1)


def solution(mesh):
    placed = (P("rows", None), P("ctr", None), P("rows"), P("rows"))
    return jax.shard_map(
        local,
        mesh=mesh,
        in_specs=placed,
        out_specs=(P(("rows", "ctr")), P(("ctr", "rows"), None), P(("ctr", "rows"))),
        check_vma=False,
    )
```

```python
import functools

import jax
import jax.numpy as jnp
from jax import lax
from jax.experimental import pallas as pl
from jax.experimental.pallas import tpu as pltpu
from jax.sharding import PartitionSpec as P

KO = 16
CAP = 4
LANES = 128
MESH = pl.DeviceIdType.MESH
F32 = jnp.float32
BF16 = jnp.bfloat16
CODE = jnp.int16


def iota(shape, dim):
    return lax.broadcasted_iota(jnp.int32, shape, dim)


def dot_nt(a, b):
    return lax.dot_general(a, b, (((1,), (1,)), ((), ())), preferred_element_type=F32)


def dot_nn(a, b):
    return lax.dot_general(a, b, (((1,), (0,)), ((), ())), preferred_element_type=F32)


def split3(x):
    hi = x.astype(BF16).astype(F32)
    mid = (x - hi).astype(BF16).astype(F32)
    lo = ((x - hi) - mid).astype(BF16).astype(F32)
    return [hi, mid, lo]


def weight_code(x):
    return (((x - 0.25) * (65535 / 3.75) + 0.5).astype(jnp.int32) - 32768).astype(CODE)


def code_weight(code):
    return (code.astype(jnp.int32) + 32768).astype(F32) * (3.75 / 65535) + 0.25


def cost_code(x):
    at = (jnp.log2(jnp.maximum(x, 2.0**-106)) + 106.0) * 512.0 + 0.5
    return (jnp.minimum(at, 65535.0).astype(jnp.int32) - 32768).astype(CODE)


def code_cost(code):
    return jnp.exp2((code.astype(jnp.int32) + 32768).astype(F32) * (1 / 512) - 106.0)


def spread(parts):
    stack = jnp.concatenate(parts, axis=0)
    block = iota(stack.shape, 0) & 7
    return jnp.concatenate([jnp.where(block == b, stack, 0.0) for b in range(8)], axis=1).astype(BF16)


def kernel(
    n_rows,
    n_ctr,
    points_hbm,
    centers_hbm,
    assign_hbm,
    weight_hbm,
    row_share_ref,
    centroid_ref,
    share_ref,
    points,
    centers,
    assign_ref,
    weight_ref,
    pick,
    rows_out,
    rows_in,
    min_out,
    min_in,
    ids_out,
    ids_in,
    label_out,
    label_in,
    cost_out,
    cost_in,
    wide_ids,
    labels,
    near_ref,
    load_sem,
    send_sems,
    recv_sems,
    cost_sems,
    late_sem,
    go_sem,
):
    s = lax.axis_index("rows")
    c = lax.axis_index("ctr")
    chunk = points.shape[0] // 4
    n_own = row_share_ref.shape[1]

    def row_peer(d):
        k = d >> 2
        away = ((k + 1) >> 1) * (2 * (k & 1) - 1)
        low = (s + d) & 3
        r = (((s >> 2) + away) & (n_rows // 4 - 1)) * 4 + low
        other = ((low >> 1) + (s >> 1)) & 1
        return r, c + other * (1 - 2 * (c & 1))

    def row_peers(act, unroll=False):
        if unroll:
            for d in range(n_rows - 1, 0, -1):
                act(row_peer(d))
            return

        def step(d, carry):
            act(row_peer(n_rows - d))
            return carry

        lax.fori_loop(1, n_rows, step, 0)

    half = n_ctr // 2

    def early_peers(act):
        for p in range(half):
            pl.when(p != c)(functools.partial(act, p))

    def late_peers(act):
        for p in range(half, n_ctr):
            pl.when(p != c)(functools.partial(act, p))

    barrier = pltpu.get_barrier_semaphore()
    center_load = pltpu.make_async_copy(centers_hbm, centers, load_sem.at[4])
    center_load.start()
    point_loads = []
    for q in range(4):
        part = pl.ds(q * chunk, chunk)
        load = pltpu.make_async_copy(points_hbm.at[part], points.at[part], load_sem.at[q])
        load.start()
        point_loads.append(load)
    assign_load = pltpu.make_async_copy(assign_hbm, assign_ref, load_sem.at[5])
    assign_load.start()
    weight_load = pltpu.make_async_copy(weight_hbm, weight_ref, load_sem.at[6])
    weight_load.start()

    def enter(p):
        pl.semaphore_signal(barrier, inc=1, device_id=(s, p), device_id_type=MESH)

    @pl.when(c < half)
    def _():
        early_peers(enter)
        late_peers(enter)

    row_peers(lambda to: pl.semaphore_signal(barrier, inc=1, device_id=to, device_id_type=MESH), True)

    def slots():
        assign = assign_ref[...]
        weight = weight_ref[...]
        for h in range(2):
            ids_out[h, 0] = assign[4 * h : 4 * h + 4].astype(CODE)
            ids_out[h, 1] = weight_code(weight[4 * h : 4 * h + 4])
        run = (assign >> 4) & (n_rows - 1)
        other = ((run >> 1) + lax.rem(s, 4) // 2) & 1
        run = jnp.where(assign >> 9 == c + other * (1 - 2 * lax.rem(c, 2)), run, -1)
        member = (assign & (KO - 1)).astype(F32)
        hot = [(run[b : b + 1, :] == iota((n_rows, LANES), 0)).astype(F32) for b in range(8)]
        before = jnp.concatenate(
            [
                (iota((LANES, LANES), 0) < iota((LANES, LANES), 1)).astype(F32),
                jnp.ones((LANES, LANES), F32),
            ],
            axis=1,
        ).astype(BF16)
        counted = dot_nn(jnp.concatenate(hot, axis=0).astype(BF16), before)
        carry = jnp.zeros((n_rows, LANES), F32)
        for b in range(8):
            rank = counted[b * n_rows : (b + 1) * n_rows, :LANES] + carry
            carry = carry + counted[b * n_rows : (b + 1) * n_rows, LANES:]
            rank = jnp.sum(hot[b] * rank, axis=0, keepdims=True).astype(jnp.int32)
            here = run[b : b + 1, :]
            code = jnp.where(here >= 0, here * CAP + rank, -1)
            lanes = pl.ds(b * LANES, LANES)
            pick[0:LANES, lanes] = (iota((LANES, LANES), 0) == code).astype(F32).astype(BF16)
            at = iota((2 * LANES, LANES), 0)
            at = (at >> 3) * CAP + (at & (CAP - 1))
            pick[LANES : 3 * LANES, lanes] = (at == code).astype(F32).astype(BF16)

        traits = spread([member + 1.0] + split3(weight))
        label_out[...] = jnp.sum(dot_nt(traits[0:8], pick[0:LANES, :]), axis=0, keepdims=True) - 1.0

        row_weight = jnp.sum(dot_nt(pick[LANES : 3 * LANES, :], traits[8:32]), axis=1, keepdims=True)
        odd = (iota((2 * LANES, 256), 0) >> 2) & 1
        tiles = []
        for t in range(2):
            low = dot_nn(pick[LANES : 3 * LANES, :], points[:, pl.ds(2 * t * 256, 256)])
            high = dot_nn(pick[LANES : 3 * LANES, :], points[:, pl.ds((2 * t + 1) * 256, 256)])
            tiles.append((jnp.where(odd == 0, low, high) * row_weight).reshape(n_rows, 8, 256))
        rows_out[...] = jnp.concatenate(tiles, axis=1).astype(BF16)

    assign_load.wait()
    weight_load.wait()
    def loaded(first, last):
        for load in point_loads[first:last]:
            load.wait()

    @pl.when(c < half)
    def _():
        loaded(0, 4)
        slots()

    pl.when(c >= half)(functools.partial(loaded, 0, 2))

    center_load.wait()
    wide = centers[...].astype(F32)
    half_norm = 0.5 * jnp.sum(wide * wide, axis=1, keepdims=True)
    for q in range(4):
        if q == 2:
            pl.when(c >= half)(functools.partial(loaded, 2, 4))
        some = points[q * chunk : (q + 1) * chunk, :]
        least = jnp.min(half_norm - dot_nt(centers[...], some), axis=0, keepdims=True)
        for k in range(2):
            min_out[2 * q + k : 2 * q + k + 1, :] = least[:, k * LANES : (k + 1) * LANES]

    pl.semaphore_wait(barrier, n_rows + half - 2 + c // half)

    def copy(src, dst, i, recv, device):
        return pltpu.make_async_remote_copy(
            src, dst, send_sems.at[i], recv, device_id=device, device_id_type=MESH
        )

    def wait_all(ref, count, sem):
        whole = ref.at[pl.ds(0, count)]
        pltpu.make_async_copy(whole, whole, sem).wait()

    def send_min(p):
        copy(min_out, min_in.at[c], 0, recv_sems.at[0], (s, p)).start()

    def tell_late(p):
        pl.semaphore_signal(late_sem, inc=1, device_id=(s, p), device_id_type=MESH)

    early_peers(send_min)

    @pl.when(c >= half)
    def _():
        early_peers(tell_late)
        slots()

    def send_half(src, dst, i):
        def send(to):
            h = to[0] & 1
            copy(src.at[h], dst.at[h, s], i, recv_sems.at[i], to).start()

        row_peers(send)

    core = s & 1
    send_half(ids_out, ids_in, 1)
    row_peers(lambda to: copy(label_out, label_in.at[s], 3, recv_sems.at[3], to).start())
    row_peers(lambda to: copy(rows_out.at[to[0]], rows_in.at[s], 4, recv_sems.at[4], to).start())
    min_in[c] = min_out[...]
    ids_in[core, s] = ids_out[core]
    label_in[s] = label_out[...]
    rows_in[s] = rows_out[s]

    for q in range(4):
        wide = points[q * chunk : (q + 1) * chunk, :].astype(F32)
        wide = wide * wide
        total = wide[:, 0:LANES]
        for k in range(1, 8):
            total = total + wide[:, k * LANES : (k + 1) * LANES]
        norm = jnp.sum(total.T, axis=0, keepdims=True)
        for k in range(2):
            near_ref[2 * q + k : 2 * q + k + 1, :] = norm[:, k * LANES : (k + 1) * LANES]

    @pl.when(c < half)
    def _():
        pl.semaphore_wait(late_sem, half)
        mirror = n_ctr - 2 - 2 * (c // 2) + c % 2
        pl.semaphore_signal(go_sem, inc=1, device_id=(s, mirror), device_id_type=MESH)
        late_peers(send_min)

    @pl.when(c >= half)
    def _():
        pl.semaphore_wait(go_sem, 1)
        late_peers(send_min)

    wait_all(min_in, n_ctr - 1, recv_sems.at[0])
    near = near_ref[...] + 2.0 * jnp.min(min_in[...], axis=0)
    near_ref[...] = near
    cost = near * weight_ref[...]
    cost_out[...] = cost_code(cost)
    row_peers(lambda to: copy(cost_out, cost_in.at[s], 5, cost_sems.at[s], to).start(), True)
    cost_in[s] = cost_out[...]

    side = iota((LANES, LANES), 0) == iota((LANES, LANES), 1)
    own = assign_ref[pl.ds(c // 2, 1), :].astype(F32)
    own = jnp.sum(jnp.where(side, own, 0.0), axis=1, keepdims=True)
    own = jnp.where(c % 2 == 0, own[:n_own], own[n_own : 2 * n_own])
    first = (c * n_rows + s) * KO
    own = jnp.concatenate([own.astype(jnp.int32), first + iota((KO, 1), 0)], axis=0)
    own = jnp.broadcast_to(own, (n_own + KO, LANES))

    def add(r, values, sums):
        total, each = sums
        ids = wide_ids[r]
        for b in range(8):
            each = each + jnp.where(ids[b : b + 1, :] == own, values[b : b + 1, :], 0.0)
        return total + values, each

    zeros = (jnp.zeros((8, LANES), F32), jnp.zeros(own.shape, F32))

    def add_weight(r, sums):
        for h in range(2):
            wide_ids[r, 4 * h : 4 * h + 4] = ids_in[h, r, 0].astype(jnp.int32)
        return add(r, code_weight(jnp.concatenate([ids_in[0, r, 1], ids_in[1, r, 1]], axis=0)), sums)

    wait_all(ids_in.at[0], n_rows - 1, recv_sems.at[1])
    partner = (s + 1 - 2 * core, c)
    give = copy(ids_in.at[core], ids_in.at[core], 2, recv_sems.at[2], partner)
    give.start()
    give.wait_recv()
    weight_sum, size = lax.fori_loop(0, n_rows, add_weight, zeros)
    weight_sum = jnp.sum(weight_sum, keepdims=True)
    size = jnp.maximum(jnp.sum(size, axis=1, keepdims=True), 1.0)

    wait_all(label_in, n_rows - 1, recv_sems.at[3])
    for r in range(n_rows):
        labels[r : r + 1, :] = label_in[r]
    lane = iota((LANES, n_rows * KO), 1)
    at = iota((LANES, n_rows * KO), 0)
    place = (at == s * CAP + (lane & (CAP - 1))).astype(F32).astype(BF16)
    ids = dot_nn(labels[...].astype(BF16), place)
    slab = iota((n_rows, n_rows * KO), 0) == iota((n_rows, n_rows * KO), 1) // KO
    ids = jnp.sum(jnp.where(slab, ids, 0.0), axis=0, keepdims=True).astype(jnp.int32)
    at = iota((4 * KO, n_rows * KO), 0)
    quarter = (iota((4 * KO, n_rows * KO), 1) & (KO - 1)) >> 2
    member = ((at & (KO - 1)) == ids) & ((at >> 4) == quarter)
    member = member.astype(F32).astype(BF16)
    wait_all(rows_in, n_rows - 1, recv_sems.at[4])
    coord = dot_nn(member, rows_in[...].reshape(n_rows * KO, 256))
    for q in range(4):
        centroid_ref[:, q * 256 : (q + 1) * 256] = coord[q * KO : (q + 1) * KO, :] / size[n_own:]

    def add_costs(first, count, sums):
        slabs = [row_peer(first + j)[0] for j in range(count)]
        for r in slabs:
            pltpu.make_async_copy(cost_in.at[r], cost_in.at[r], cost_sems.at[r]).wait()
        for r in slabs:
            sums = add(r, code_cost(cost_in[r]), sums)
        return sums

    sums = add_costs(1, 3, add(s, cost, zeros))
    cost_sum, own_cost = lax.fori_loop(1, n_rows // 4, lambda k, sums: add_costs(4 * k, 4, sums), sums)
    mean = jnp.sum(cost_sum, keepdims=True) / weight_sum
    share = jnp.sum(own_cost, axis=1, keepdims=True) / (size * mean)
    diagonal = iota(own.shape, 0) == iota(own.shape, 1)
    share = jnp.sum(jnp.where(diagonal, share, 0.0), axis=0, keepdims=True)
    share_ref[...] = share[:, n_own : n_own + KO]
    near = near_ref[pl.ds(c // 2, 1), :]
    near = jnp.where(c % 2 == 0, near[:, :n_own], near[:, n_own : 2 * n_own])
    row_share_ref[...] = near / mean + 2.0 * share[:, :n_own]

    wait_all(min_in, n_ctr - 1, send_sems.at[0])
    wait_all(ids_in.at[0], n_rows - 1, send_sems.at[1])
    give.wait_send()
    wait_all(label_in, n_rows - 1, send_sems.at[3])
    wait_all(rows_in, n_rows - 1, send_sems.at[4])
    wait_all(cost_in, n_rows - 1, send_sems.at[5])


def deliver(*refs):
    n = len(refs) // 2
    copies = [pltpu.make_async_copy(refs[i], refs[n + i], refs[-1].at[i]) for i in range(n)]
    for copy in copies:
        copy.start()
    for copy in copies:
        copy.wait()


def local(points, centers, assignment, row_weight):
    slab_rows, width = points.shape
    block = centers.shape[0]
    n_rows = lax.axis_size("rows")
    n_ctr = lax.axis_size("ctr")
    vmem = pl.BlockSpec(memory_space=pltpu.VMEM)
    hbm = pl.BlockSpec(memory_space=pltpu.HBM)
    row_share, centroid, share = pl.pallas_call(
        functools.partial(kernel, n_rows, n_ctr),
        out_shape=(
            pltpu.VMEM((1, slab_rows // n_ctr), F32),
            pltpu.VMEM((KO, width), F32),
            pltpu.VMEM((1, KO), F32),
        ),
        in_specs=[hbm, hbm, hbm, hbm],
        out_specs=(vmem, vmem, vmem),
        scratch_shapes=[
            pltpu.VMEM((slab_rows, width), BF16),
            pltpu.VMEM((block, width), BF16),
            pltpu.VMEM((8, LANES), jnp.int32),
            pltpu.VMEM((8, LANES), F32),
            pltpu.VMEM((3 * LANES, slab_rows), BF16),
            pltpu.VMEM((n_rows, 16, 256), BF16),
            pltpu.VMEM((n_rows, 16, 256), BF16),
            pltpu.VMEM((8, LANES), F32),
            pltpu.VMEM((n_ctr, 8, LANES), F32),
            pltpu.VMEM((2, 2, 4, LANES), CODE),
            pltpu.VMEM((2, n_rows, 2, 4, LANES), CODE),
            pltpu.VMEM((1, LANES), F32),
            pltpu.VMEM((n_rows, 1, LANES), F32),
            pltpu.VMEM((8, LANES), CODE),
            pltpu.VMEM((n_rows, 8, LANES), CODE),
            pltpu.VMEM((n_rows, 8, LANES), jnp.int32),
            pltpu.VMEM((n_rows, LANES), F32),
            pltpu.VMEM((8, LANES), F32),
            pltpu.SemaphoreType.DMA((7,)),
            pltpu.SemaphoreType.DMA((6,)),
            pltpu.SemaphoreType.DMA((5,)),
            pltpu.SemaphoreType.DMA((n_rows,)),
            pltpu.SemaphoreType.REGULAR,
            pltpu.SemaphoreType.REGULAR,
        ],
        compiler_params=pltpu.CompilerParams(
            collective_id=0, has_side_effects=True, vmem_limit_bytes=48 * 1024 * 1024
        ),
        cost_estimate=pl.CostEstimate(
            flops=2 * slab_rows * width * (block + 3 * LANES),
            bytes_accessed=2 * (slab_rows + block) * width,
            transcendentals=0,
        ),
    )(*(pltpu.with_memory_space_constraint(x, pltpu.HBM) for x in (points, centers, assignment.reshape(8, LANES), row_weight.reshape(8, LANES))))
    made = (row_share, centroid, share)
    row_share, centroid, share = pl.pallas_call(
        deliver,
        out_shape=tuple(jax.ShapeDtypeStruct(x.shape, x.dtype) for x in made),
        in_specs=[vmem] * 3,
        out_specs=(hbm,) * 3,
        scratch_shapes=[pltpu.SemaphoreType.DMA((3,))],
        compiler_params=pltpu.CompilerParams(vmem_limit_bytes=4 * 1024 * 1024),
    )(*made)
    return row_share.reshape(-1), centroid, share.reshape(-1)


def solution(mesh):
    placed = (P("rows", None), P("ctr", None), P("rows"), P("rows"))
    return jax.shard_map(
        local,
        mesh=mesh,
        in_specs=placed,
        out_specs=(P(("rows", "ctr")), P(("ctr", "rows"), None), P(("ctr", "rows"))),
        check_vma=False,
    )
```
